32 devices in a mesh: dp: 4 (over y, x), fsdp: 4 (over z), tensor: 2 (over core).
Axes of the slice: x: 2, y: 2, z: 4, core: 2. Of those that a mesh axis runs over, the one named last changes fastest.
Arguments:
- momentum: bfloat16 [4, 8192, 8192], P('dp', 'fsdp', 'tensor'), may hold values from -24 to 24
- gradient: bfloat16 [4, 8192, 8192], P('dp', 'fsdp', 'tensor'), may hold values from -4 to 4
- factor: float32 [8192, 256], P('tensor'), may hold values from -6 to 6
Outputs:
- new_momentum: float32 [4, 8192, 8192], P('dp', 'fsdp', 'tensor')
- step_direction: bfloat16 [8192, 8192], P('fsdp', 'tensor')
- new_factor: float32 [8192, 256], P('tensor')
The draws below stay inside these ranges and needn't reach their ends.
All inputs are finite; a program needn't handle non-finite values.
Results may differ from the reference program's by a relative error of at most 0.0065.
Values may be sent and summed in bfloat16 or wider, within the bound.
No kernel may reach another device: no remote copies, remote signals or barrier semaphores. Data moves between devices by JAX's collectives and lax.ppermute only.
A program may use at most 192 MiB of HBM per device.

```python
import jax
import jax.numpy as jnp
from jax import lax

ROWS = 8192
COLS = 8192
RANK = 256
REPLICAS = 4


def rising_scale(key, count, start, finish, rough):
    trend = jnp.linspace(jnp.log(start), jnp.log(finish), count).astype(jnp.float32)
    jitter = jax.random.uniform(key, (count,), jnp.float32, jnp.log(rough), 0.0)
    return jnp.exp(trend + jitter)


def draw_momentum(key, part):
    low_rank = max(RANK // 2, 1)
    key_rows = jax.random.fold_in(key, 21)
    key_cols = jax.random.fold_in(key, 22)
    key_left = jax.random.fold_in(key, 23)
    key_right = jax.random.fold_in(key, 24)
    key_weights = jax.random.fold_in(key, 25)
    key_noise = jax.random.fold_in(key, 26)
    key_replica = jax.random.fold_in(key, 27)
    row_scale = rising_scale(key_rows, ROWS, 0.5, 4.0, 0.5)
    col_scale = rising_scale(key_cols, COLS, 0.5, 4.0, 0.5)
    left_basis = jax.random.normal(key_left, (ROWS, low_rank), jnp.float32)
    right_basis = jax.random.normal(key_right, (COLS, low_rank), jnp.float32)
    noise = jax.random.normal(key_noise, (REPLICAS, ROWS, COLS), jnp.float32)
    replica_scale = jnp.exp(jnp.linspace(0.0, jnp.log(3.0), REPLICAS).astype(jnp.float32) + jax.random.uniform(key_replica, (REPLICAS,), jnp.float32, -0.1, 0.1))
    weights = jnp.exp(jax.random.uniform(key_weights, (low_rank,), jnp.float32, 0.0, jnp.log(2.0)))
    shared = jnp.dot(left_basis * weights[None, :], right_basis.T) / jnp.sqrt(jnp.sum(weights * weights))
    values = shared[None] + noise
    values = 0.15 * values * replica_scale[:, None, None] * row_scale[None, :, None] * col_scale[None, None, :]
    return jnp.clip(values, -24.0, 24.0).astype(jnp.bfloat16)


def draw_gradient(key, part):
    key_rows = jax.random.fold_in(key, 11)
    key_cols = jax.random.fold_in(key, 12)
    key_own = jax.random.fold_in(key, 13)
    row_scale = jnp.exp(jax.random.uniform(key_rows, (1, ROWS, 1), jnp.float32, jnp.log(0.3), jnp.log(3.0)))
    col_scale = jnp.exp(jax.random.uniform(key_cols, (1, 1, COLS), jnp.float32, jnp.log(0.3), jnp.log(3.0)))
    values = jax.random.truncated_normal(key_own, -4.0, 4.0, (REPLICAS, ROWS, COLS), jnp.float32)
    return (0.1 * values * row_scale * col_scale).astype(jnp.bfloat16)


def shard_levels(rng, shape, pieces, least, largest):
    def one(dim, shards_of):
        heights = jax.random.uniform(jax.random.fold_in(jax.random.fold_in(rng, 6), dim), (shards_of,), jnp.float32, least / len(pieces), largest / len(pieces))
        return jnp.repeat(jnp.exp(heights), shape[dim] // shards_of).reshape((-1,) + (1,) * (len(shape) - dim - 1))

    gain = one(*pieces[0])
    for cut in pieces[1:]:
        gain = gain * one(*cut)
    return gain


def scatter_about(rng, shape, deviation, limit, shards=(), held_as=jnp.bfloat16):
    loudness = shard_levels(rng, shape, shards, -0.22, 0.18) if shards else 1.0
    array = jax.random.normal(rng, shape, jnp.float32) * deviation * loudness
    return jnp.minimum(jnp.maximum(array, -limit), limit).astype(held_as)


def setup_inputs(seed: int = 0) -> dict:
    arg_keys = jax.random.split(jax.random.key(seed), 4)
    return {
        "momentum": draw_momentum(jax.random.fold_in(arg_keys[3], 71), 0),
        "gradient": draw_gradient(jax.random.fold_in(arg_keys[3], 71), 0),
        "factor": scatter_about(arg_keys[2], (COLS, RANK), 1.0, 6.0, ((0, 2),), jnp.float32),
    }


def reference(momentum, gradient, factor):
    highest = lax.Precision.HIGHEST
    factor_low = factor.astype(jnp.bfloat16)
    left = jnp.zeros((ROWS, RANK), jnp.float32)
    for replica in range(REPLICAS):
        left = left + jnp.dot(momentum[replica].astype(jnp.float32), factor_low.astype(jnp.float32), preferred_element_type=jnp.float32)
        left = left + jnp.dot(gradient[replica].astype(jnp.float32), factor_low.astype(jnp.float32), preferred_element_type=jnp.float32)
    left = left / REPLICAS
    gram = jnp.dot(left.T, left, precision=highest)
    lower = jnp.linalg.cholesky(gram)
    ortho = jax.scipy.linalg.solve_triangular(lower, left.T, lower=True).T
    ortho_low = ortho.astype(jnp.bfloat16)
    right = jnp.zeros((COLS, RANK), jnp.float32)
    for replica in range(REPLICAS):
        right = right + jnp.dot(momentum[replica].T.astype(jnp.float32), ortho_low.astype(jnp.float32), preferred_element_type=jnp.float32)
        right = right + jnp.dot(gradient[replica].T.astype(jnp.float32), ortho_low.astype(jnp.float32), preferred_element_type=jnp.float32)
    right = right / REPLICAS
    square_sums = lax.optimization_barrier(jnp.sum(right * right, axis=0))
    new_factor = right / jnp.sqrt(square_sums / COLS + 1e-06)
    right_low = right.astype(jnp.bfloat16)
    feedback = jnp.dot(ortho_low.astype(jnp.float32), right_low.T.astype(jnp.float32), preferred_element_type=jnp.float32)
    new_momentum = jnp.stack([momentum[replica].astype(jnp.float32) + gradient[replica].astype(jnp.float32) - 0.05 * feedback for replica in range(REPLICAS)])
    step_scale = jnp.sqrt(jnp.float32(ROWS / RANK))
    factor_next_low = new_factor.astype(jnp.bfloat16)
    step_direction = (step_scale * jnp.dot(ortho_low.astype(jnp.float32), factor_next_low.T.astype(jnp.float32), preferred_element_type=jnp.float32)).astype(jnp.bfloat16)
    return (new_momentum, step_direction, new_factor)
```

```python
import functools

import jax
import jax.numpy as jnp
from jax import lax
from jax.experimental import pallas as pl
from jax.experimental.pallas import tpu as pltpu
from jax.sharding import PartitionSpec as P

F32 = jnp.float32
LOW = jnp.bfloat16
LANES = 128
COLS_OVER = (((0,), (0,)), ((), ()))


def inverse_factor_kernel(panel, group, gram_ref, out_ref, work_ref):
    n = gram_ref.shape[0]
    work_ref[...] = jnp.zeros_like(work_ref)
    out_ref[...] = jnp.zeros_like(out_ref)
    rows = lax.broadcasted_iota(jnp.int32, (panel, LANES), 0)
    lanes = lax.broadcasted_iota(jnp.int32, (panel, LANES), 1)
    product = functools.partial(
        lax.dot_general,
        dimension_numbers=COLS_OVER,
        precision=lax.Precision.HIGHEST,
        preferred_element_type=F32,
    )
    for start in range(0, n, panel):
        base = start // LANES * LANES
        wide = base + LANES
        upper = gram_ref[start : start + panel, base:n]
        if start:
            before = work_ref[0:start, start : start + panel]
            upper = upper - product(before, work_ref[0:start, base:n])
            inverse = -product(before, work_ref[0:start, n : n + wide])
            inverse = [inverse[:, c : c + LANES] for c in range(0, wide, LANES)]
        else:
            inverse = [jnp.zeros((panel, LANES), F32)]
        inverse[-1] = inverse[-1] + (lanes == rows + (start - base)).astype(F32)
        upper = [upper[:, c : c + LANES] for c in range(0, n - base, LANES)]
        pivots = jnp.ones((panel, LANES), F32)
        for first in range(0, panel, group):
            lane = start - base + first
            columns = [
                jnp.broadcast_to(upper[0][:, lane + q : lane + q + 1], (panel, LANES))
                for q in range(group)
            ]
            factors = []
            for j in range(group):
                r = first + j
                pivot = columns[j][r : r + 1, :]
                pivots = jnp.where(rows == r, jnp.broadcast_to(pivot, rows.shape), pivots)
                factors.append(jnp.where(rows > r, columns[j] * (1.0 / pivot), 0.0))
                for q in range(j + 1, group):
                    columns[q] = columns[q] - factors[j] * columns[q][r : r + 1, :]
            for j in range(group):
                r = first + j
                upper = [x - factors[j] * x[r : r + 1, :] for x in upper]
                inverse = [x - factors[j] * x[r : r + 1, :] for x in inverse]
        scale = lax.rsqrt(pivots)
        for t, x in enumerate(upper):
            at = base + t * LANES
            work_ref[start : start + panel, at : at + LANES] = x * scale
        for t, x in enumerate(inverse):
            at = t * LANES
            work_ref[start : start + panel, n + at : n + at + LANES] = x * scale
            out_ref[start : start + panel, at : at + LANES] = x * scale


def inverse_factor(gram):
    n = gram.shape[0]
    return pl.pallas_call(
        functools.partial(inverse_factor_kernel, 32, 16),
        out_shape=jax.ShapeDtypeStruct((n, n), F32),
        scratch_shapes=[pltpu.VMEM((n, 2 * n), F32)],
        cost_estimate=pl.CostEstimate(flops=2 * n**3, bytes_accessed=8 * n * n, transcendentals=n),
    )(gram)


def bits_of(axis):
    return range(lax.axis_size(axis).bit_length() - 1)


def swap(x, axis, mask):
    size = lax.axis_size(axis)
    return lax.ppermute(x, axis, [(i, i ^ mask) for i in range(size)])


def halve(x, axis, bit, dtype):
    mine = (lax.axis_index(axis) >> bit) & 1
    halves = x.reshape(2, x.shape[0] // 2, x.shape[1])
    kept = lax.dynamic_index_in_dim(halves, mine, 0, False)
    sent = lax.dynamic_index_in_dim(halves, 1 - mine, 0, False)
    return kept + swap(sent.astype(dtype), axis, 1 << bit).astype(F32)


def unhalve(x, axis, bit):
    mine = (lax.axis_index(axis) >> bit) & 1
    other = swap(x, axis, 1 << bit)
    return jnp.where(mine == 0, jnp.concatenate([x, other]), jnp.concatenate([other, x]))


def add_both(x, axis, bit):
    low = x.astype(LOW)
    return low.astype(F32) + swap(low, axis, 1 << bit).astype(F32)


def tree_sum(terms):
    while len(terms) > 1:
        terms = [terms[i] + terms[i + 1] for i in range(0, len(terms), 2)]
    return terms[0]


def sum_left(partial):
    for bit in bits_of("tensor"):
        partial = halve(partial, "tensor", bit, F32)
    half = partial.shape[0] // 2
    parts = [partial[:half], partial[half:]]
    bits = list(bits_of("dp"))
    for k in range(len(bits)):
        parts = [
            add_both(part, "dp", bits[(k + turn) % len(bits)]) for turn, part in enumerate(parts)
        ]
    low = (jnp.concatenate(parts) / lax.axis_size("dp")).astype(LOW)
    for bit in reversed(bits_of("tensor")):
        low = unhalve(low, "tensor", bit)
    return low


def sum_gram(gram):
    shards = lax.axis_size("tensor")
    count = gram.shape[0] // shards
    part = lax.dynamic_slice_in_dim(gram, lax.axis_index("tensor") * count, count, 0)
    part = tree_sum([part] + [swap(part, "fsdp", k) for k in range(1, lax.axis_size("fsdp"))])
    for bit in bits_of("tensor"):
        part = unhalve(part, "tensor", bit)
    return part


def scatter_right(partial):
    half = partial.shape[0] // 2
    parts = [partial[:half], partial[half:]]
    bits = list(bits_of("dp"))
    for k in range(len(bits)):
        parts = [
            halve(part, "dp", bits[(k + turn) % len(bits)], LOW) for turn, part in enumerate(parts)
        ]
    size = lax.axis_size("fsdp")
    index = lax.axis_index("fsdp")
    rank = partial.shape[1]
    split = jnp.stack([part.reshape(size, -1, rank) for part in parts], axis=1)
    own = lax.dynamic_index_in_dim(split, index, 0, False)
    terms = [own]
    for k in range(1, size):
        sent = lax.dynamic_index_in_dim(split, index ^ k, 0, False).astype(LOW)
        terms.append(swap(sent, "fsdp", k).astype(F32))
    return tree_sum(terms)


def gather_right(low):
    size = lax.axis_size("fsdp")
    index = lax.axis_index("fsdp")
    rank = low.shape[-1]
    blocks = jnp.stack([low] + [swap(low, "fsdp", k) for k in range(1, size)])
    for bit in bits_of("fsdp"):
        turned = blocks.reshape((-1, 2, 1 << bit) + low.shape)[:, ::-1].reshape(blocks.shape)
        blocks = jnp.where((index >> bit) & 1, turned, blocks)
    parts = [blocks[:, 0].reshape(-1, rank), blocks[:, 1].reshape(-1, rank)]
    bits = list(bits_of("dp"))
    for k in reversed(range(len(bits))):
        parts = [
            unhalve(part, "dp", bits[(k + turn) % len(bits)]) for turn, part in enumerate(parts)
        ]
    return jnp.concatenate(parts)


def transposed_product(block, low):
    return lax.dot_general(block, low, COLS_OVER, preferred_element_type=F32)


def local(momentum, gradient, factor):
    high = lax.Precision.HIGH
    replicas = lax.axis_size("dp")
    moment = momentum[0]
    change = gradient[0]
    all_rows = moment.shape[0] * lax.axis_size("fsdp")
    all_cols = moment.shape[1] * lax.axis_size("tensor")
    factor_low = factor.astype(LOW)
    left_low = sum_left(
        jnp.dot(moment, factor_low, preferred_element_type=F32)
        + jnp.dot(change, factor_low, preferred_element_type=F32)
    )
    gram = sum_gram(transposed_product(left_low, left_low))
    mixed = transposed_product(moment, left_low) + transposed_product(change, left_low)
    inverse = inverse_factor(gram)
    ortho_low = jnp.dot(left_low.astype(F32), inverse.T, precision=high).astype(LOW)
    right = scatter_right(jnp.dot(mixed, inverse.T, precision=high)) / replicas
    right_low = gather_right(right.astype(LOW))
    right = right_low.astype(F32)
    square_sums = jnp.sum(right * right, axis=0)
    for bit in bits_of("tensor"):
        square_sums = square_sums + swap(square_sums, "tensor", 1 << bit)
    new_factor = right / jnp.sqrt(square_sums / all_cols + 1e-06)
    feedback = jnp.dot(ortho_low, right_low.T, preferred_element_type=F32)
    new_momentum = (moment.astype(F32) + change.astype(F32) - 0.05 * feedback)[None]
    step_scale = jnp.sqrt(F32(all_rows / factor.shape[1]))
    step_direction = (
        step_scale
        * jnp.dot(ortho_low, new_factor.astype(LOW).T, preferred_element_type=F32)
    ).astype(LOW)
    return (new_momentum, step_direction, new_factor)


def solution(mesh):
    in_specs = (P("dp", "fsdp", "tensor"), P("dp", "fsdp", "tensor"), P("tensor", None))
    out_specs = (P("dp", "fsdp", "tensor"), P("fsdp", "tensor"), P("tensor", None))
    return jax.shard_map(local, mesh=mesh, in_specs=in_specs, out_specs=out_specs, check_vma=False)
```

```python
import functools

import jax
import jax.numpy as jnp
from jax import lax
from jax.experimental import pallas as pl
from jax.experimental.pallas import tpu as pltpu
from jax.sharding import PartitionSpec as P

F32 = jnp.float32
LOW = jnp.bfloat16
LANES = 128
COLS_OVER = (((0,), (0,)), ((), ()))


def inverse_factor_kernel(panel, group, gram_ref, out_ref, work_ref):
    n = gram_ref.shape[0]
    work_ref[...] = jnp.zeros_like(work_ref)
    out_ref[...] = jnp.zeros_like(out_ref)
    rows = lax.broadcasted_iota(jnp.int32, (panel, LANES), 0)
    lanes = lax.broadcasted_iota(jnp.int32, (panel, LANES), 1)
    product = functools.partial(
        lax.dot_general,
        dimension_numbers=COLS_OVER,
        precision=lax.Precision.HIGHEST,
        preferred_element_type=F32,
    )
    for start in range(0, n, panel):
        base = start // LANES * LANES
        wide = base + LANES
        upper = gram_ref[start : start + panel, base:n]
        if start:
            before = work_ref[0:start, start : start + panel]
            upper = upper - product(before, work_ref[0:start, base:n])
            inverse = -product(before, work_ref[0:start, n : n + wide])
            inverse = [inverse[:, c : c + LANES] for c in range(0, wide, LANES)]
        else:
            inverse = [jnp.zeros((panel, LANES), F32)]
        inverse[-1] = inverse[-1] + (lanes == rows + (start - base)).astype(F32)
        upper = [upper[:, c : c + LANES] for c in range(0, n - base, LANES)]
        pivots = jnp.ones((panel, LANES), F32)
        for first in range(0, panel, group):
            lane = start - base + first
            columns = [
                jnp.broadcast_to(upper[0][:, lane + q : lane + q + 1], (panel, LANES))
                for q in range(group)
            ]
            factors = []
            for j in range(group):
                r = first + j
                pivot = columns[j][r : r + 1, :]
                pivots = jnp.where(rows == r, jnp.broadcast_to(pivot, rows.shape), pivots)
                factors.append(jnp.where(rows > r, columns[j] * (1.0 / pivot), 0.0))
                for q in range(j + 1, group):
                    columns[q] = columns[q] - factors[j] * columns[q][r : r + 1, :]
            for j in range(group):
                r = first + j
                upper = [x - factors[j] * x[r : r + 1, :] for x in upper]
                inverse = [x - factors[j] * x[r : r + 1, :] for x in inverse]
        scale = lax.rsqrt(pivots)
        for t, x in enumerate(upper):
            at = base + t * LANES
            work_ref[start : start + panel, at : at + LANES] = x * scale
        for t, x in enumerate(inverse):
            at = t * LANES
            work_ref[start : start + panel, n + at : n + at + LANES] = x * scale
            out_ref[start : start + panel, at : at + LANES] = x * scale


def apply_kernel(panel, group, gram_ref, high_ref, low_ref, inverse_ref, right_ref, work_ref):
    inverse_factor_kernel(panel, group, gram_ref, inverse_ref, work_ref)
    inverse = inverse_ref[...]
    inverse_high = inverse.astype(LOW)
    inverse_low = (inverse - inverse_high.astype(F32)).astype(LOW)
    width = tile_of(high_ref.shape[1])
    for at in range(0, high_ref.shape[1], width):
        high = high_ref[:, at : at + width]
        low = low_ref[:, at : at + width]
        right_ref[:, at : at + width] = (
            jnp.dot(inverse_high, low, preferred_element_type=F32)
            + jnp.dot(inverse_low, high, preferred_element_type=F32)
        ) + jnp.dot(inverse_high, high, preferred_element_type=F32)


def apply_inverse(gram, high, low):
    n, columns = high.shape
    return pl.pallas_call(
        functools.partial(apply_kernel, 32, 16),
        out_shape=(
            jax.ShapeDtypeStruct((n, n), F32),
            jax.ShapeDtypeStruct((n, columns), F32),
        ),
        scratch_shapes=[pltpu.VMEM((n, 2 * n), F32)],
        compiler_params=pltpu.CompilerParams(vmem_limit_bytes=24 << 20),
        cost_estimate=pl.CostEstimate(
            flops=40 * n * n * columns, bytes_accessed=8 * n * columns, transcendentals=n
        ),
    )(gram, high, low)


def tile_of(size):
    return 256 if size % 256 == 0 else LANES


def left_kernel(moment_ref, change_ref, factor_ref, out_ref):
    factor = factor_ref[...]
    out_ref[...] = jnp.dot(moment_ref[...], factor, preferred_element_type=F32) + jnp.dot(
        change_ref[...], factor, preferred_element_type=F32
    )


def left_product(moment, change, factor_low):
    rows, columns = moment.shape
    rank = factor_low.shape[1]
    tile = LANES
    return pl.pallas_call(
        left_kernel,
        grid=(rows // tile,),
        in_specs=[
            pl.BlockSpec((tile, columns), lambda i: (i, 0)),
            pl.BlockSpec((tile, columns), lambda i: (i, 0)),
            pl.BlockSpec((columns, rank), lambda i: (0, 0)),
        ],
        out_specs=pl.BlockSpec((tile, rank), lambda i: (i, 0)),
        out_shape=jax.ShapeDtypeStruct((rows, rank), F32),
        compiler_params=pltpu.CompilerParams(vmem_limit_bytes=24 << 20),
        cost_estimate=pl.CostEstimate(
            flops=4 * rows * columns * rank,
            bytes_accessed=4 * rows * columns,
            transcendentals=0,
        ),
    )(moment, change, factor_low)


def mixed_kernel(left_ref, moment_ref, change_ref, high_ref, low_ref):
    left = left_ref[...]
    mixed = jnp.dot(left, moment_ref[...], preferred_element_type=F32) + jnp.dot(
        left, change_ref[...], preferred_element_type=F32
    )
    high = mixed.astype(LOW)
    high_ref[...] = high
    low_ref[...] = (mixed - high.astype(F32)).astype(LOW)


def mixed_product(left_turned, moment, change):
    rows, columns = moment.shape
    rank = left_turned.shape[0]
    tile = tile_of(columns)
    return pl.pallas_call(
        mixed_kernel,
        grid=(columns // tile,),
        in_specs=[
            pl.BlockSpec((rank, rows), lambda j: (0, 0)),
            pl.BlockSpec((rows, tile), lambda j: (0, j)),
            pl.BlockSpec((rows, tile), lambda j: (0, j)),
        ],
        out_specs=[pl.BlockSpec((rank, tile), lambda j: (0, j))] * 2,
        out_shape=[jax.ShapeDtypeStruct((rank, columns), LOW)] * 2,
        compiler_params=pltpu.CompilerParams(vmem_limit_bytes=24 << 20),
        cost_estimate=pl.CostEstimate(
            flops=4 * rows * columns * rank,
            bytes_accessed=4 * rows * columns,
            transcendentals=0,
        ),
    )(left_turned, moment, change)


def feedback_kernel(place_ref, ortho_ref, right_ref, moment_ref, change_ref, *refs):
    feedback = jnp.dot(ortho_ref[...], right_ref[0], preferred_element_type=F32)
    refs[-1][0] = moment_ref[0].astype(F32) + change_ref[0].astype(F32) - 0.05 * feedback


def feedback_columns(places, ortho_low, pieces, momentum, gradient, written):
    count, rank, width = pieces.shape
    _, rows, columns = momentum.shape
    tile = tile_of(width)
    steps = width // tile

    def column(j, place):
        return (0, 0, place[j // steps] * steps + j % steps)

    block = pl.BlockSpec((1, rows, tile), column)
    specs = [
        pl.BlockSpec((rows, rank), lambda j, place: (0, 0)),
        pl.BlockSpec((1, rank, tile), lambda j, place: (j // steps, 0, j % steps)),
        block,
        block,
    ]
    operands = [places, ortho_low, pieces, momentum, gradient]
    aliases = {}
    if written is not None:
        specs.append(pl.BlockSpec(memory_space=pl.ANY))
        aliases = {len(operands): 0}
        operands.append(written)
    size = count * width
    return pl.pallas_call(
        feedback_kernel,
        grid_spec=pltpu.PrefetchScalarGridSpec(
            num_scalar_prefetch=1, grid=(count * steps,), in_specs=specs, out_specs=block
        ),
        out_shape=jax.ShapeDtypeStruct(momentum.shape, F32),
        input_output_aliases=aliases,
        compiler_params=pltpu.CompilerParams(vmem_limit_bytes=24 << 20),
        cost_estimate=pl.CostEstimate(
            flops=2 * rows * rank * size, bytes_accessed=8 * rows * size, transcendentals=0
        ),
    )(*operands)


def step_kernel(scale, place_ref, ortho_ref, right_ref, norm_ref, step_ref, factor_ref):
    factor = right_ref[0].astype(F32) / norm_ref[...]
    product = jnp.dot(ortho_ref[...], factor.astype(LOW), preferred_element_type=F32)
    step_ref[...] = (scale * product).astype(LOW)
    factor_ref[...] = factor.T


def step_outputs(places, ortho_low, pieces, norms, scale):
    count, rank, width = pieces.shape
    rows = ortho_low.shape[0]
    tile = tile_of(width)
    steps = width // tile
    columns = count * width
    return pl.pallas_call(
        functools.partial(step_kernel, scale),
        grid_spec=pltpu.PrefetchScalarGridSpec(
            num_scalar_prefetch=1,
            grid=(count * steps,),
            in_specs=[
                pl.BlockSpec((rows, rank), lambda j, place: (0, 0)),
                pl.BlockSpec((1, rank, tile), lambda j, place: (j // steps, 0, j % steps)),
                pl.BlockSpec((rank, 1), lambda j, place: (0, 0)),
            ],
            out_specs=[
                pl.BlockSpec((rows, tile), lambda j, place: (0, place[j // steps] * steps + j % steps)),
                pl.BlockSpec((tile, rank), lambda j, place: (place[j // steps] * steps + j % steps, 0)),
            ],
        ),
        out_shape=[
            jax.ShapeDtypeStruct((rows, columns), LOW),
            jax.ShapeDtypeStruct((columns, rank), F32),
        ],
        compiler_params=pltpu.CompilerParams(vmem_limit_bytes=24 << 20),
        cost_estimate=pl.CostEstimate(
            flops=2 * rows * rank * columns, bytes_accessed=2 * rows * columns, transcendentals=0
        ),
    )(places, ortho_low, pieces, norms)


def bits_of(axis):
    return range(lax.axis_size(axis).bit_length() - 1)


def swap(x, axis, mask):
    size = lax.axis_size(axis)
    return lax.ppermute(x, axis, [(i, i ^ mask) for i in range(size)])


def halve(x, axis, bit, dtype, dim):
    mine = (lax.axis_index(axis) >> bit) & 1
    size = x.shape[dim] // 2
    kept = lax.dynamic_slice_in_dim(x, mine * size, size, dim)
    sent = lax.dynamic_slice_in_dim(x, (1 - mine) * size, size, dim)
    return kept + swap(sent.astype(dtype), axis, 1 << bit).astype(F32)


def unhalve(x, axis, bit):
    mine = (lax.axis_index(axis) >> bit) & 1
    other = swap(x, axis, 1 << bit)
    return jnp.where(mine == 0, jnp.concatenate([x, other]), jnp.concatenate([other, x]))


def add_both(x, axis, bit):
    low = x.astype(LOW)
    return low.astype(F32) + swap(low, axis, 1 << bit).astype(F32)


def tree_sum(terms):
    while len(terms) > 1:
        terms = [terms[i] + terms[i + 1] for i in range(0, len(terms), 2)]
    return terms[0]


def sum_left(partial):
    for bit in bits_of("tensor"):
        partial = halve(partial, "tensor", bit, F32, 0)
    half = partial.shape[0] // 2
    parts = [partial[:half], partial[half:]]
    bits = list(bits_of("dp"))
    for k in range(len(bits)):
        parts = [
            add_both(part, "dp", bits[(k + turn) % len(bits)]) for turn, part in enumerate(parts)
        ]
    low = (jnp.concatenate(parts) / lax.axis_size("dp")).astype(LOW)
    for bit in reversed(bits_of("tensor")):
        low = unhalve(low, "tensor", bit)
    return low


def sum_gram(gram):
    shards = lax.axis_size("tensor")
    count = gram.shape[0] // shards
    part = lax.dynamic_slice_in_dim(gram, lax.axis_index("tensor") * count, count, 0)
    part = tree_sum([part] + [swap(part, "fsdp", k) for k in range(1, lax.axis_size("fsdp"))])
    for bit in bits_of("tensor"):
        part = unhalve(part, "tensor", bit)
    return part


def orders_of():
    bits = list(bits_of("dp"))
    return [bits[turn % len(bits) :] + bits[: turn % len(bits)] for turn in range(2)]


def scatter_right(partial):
    half = partial.shape[1] // 2
    parts = [partial[:, :half], partial[:, half:]]
    orders = orders_of()
    for k in range(len(orders[0])):
        parts = [
            halve(part, "dp", order[k], LOW, 1) for part, order in zip(parts, orders)
        ]
    size = lax.axis_size("fsdp")
    index = lax.axis_index("fsdp")
    width = parts[0].shape[1] // size

    def share(at):
        return jnp.concatenate(
            [lax.dynamic_slice_in_dim(part, at * width, width, 1) for part in parts], axis=1
        )

    terms = [share(index)]
    for k in range(1, size):
        terms.append(swap(share(index ^ k).astype(LOW), "fsdp", k).astype(F32))
    return tree_sum(terms)


def gather_fsdp(low):
    size = lax.axis_size("fsdp")
    index = lax.axis_index("fsdp")
    width = low.shape[1] // 2
    blocks = [low] + [swap(low, "fsdp", k) for k in range(1, size)]
    for bit in bits_of("fsdp"):
        high = ((index >> bit) & 1) == 1
        blocks = [jnp.where(high, blocks[i ^ (1 << bit)], blocks[i]) for i in range(size)]
    return [
        jnp.concatenate([b[:, :width] for b in blocks], axis=1),
        jnp.concatenate([b[:, width:] for b in blocks], axis=1),
    ]


def gather_rounds(pieces):
    index = lax.axis_index("dp")
    orders = orders_of()
    depth = len(orders[0])
    known = [{0: piece} for piece in pieces]
    rounds = []
    for r in range(depth + 1):
        new = []
        for turn, order in enumerate(orders):
            for mask in range(1 << depth):
                if mask.bit_count() != r:
                    continue
                if r:
                    bit = next(b for b in order if (mask >> b) & 1)
                    known[turn][mask] = swap(known[turn][mask ^ (1 << bit)], "dp", 1 << bit)
                place = turn << depth
                for k, b in enumerate(order):
                    place = place + ((((index ^ mask) >> b) & 1) << (depth - 1 - k))
                new.append((place, turn, mask, known[turn][mask]))
        rounds.append(new)
    return rounds


def local(momentum, gradient, factor):
    replicas = lax.axis_size("dp")
    moment = momentum[0]
    change = gradient[0]
    all_rows = moment.shape[0] * lax.axis_size("fsdp")
    all_cols = moment.shape[1] * lax.axis_size("tensor")
    left_low = sum_left(left_product(moment, change, factor.astype(LOW)))
    left_turned = left_low.T
    gram = sum_gram(jnp.dot(left_turned, left_low, preferred_element_type=F32))
    mixed_high, mixed_low = mixed_product(left_turned, moment, change)
    inverse, right = apply_inverse(gram, mixed_high, mixed_low)
    ortho_low = jnp.dot(
        left_low.astype(F32), inverse.T, precision=lax.Precision.HIGH
    ).astype(LOW)
    right = scatter_right(right) / replicas
    rounds = gather_rounds(gather_fsdp(right.astype(LOW)))
    new_momentum = None
    all_places = []
    all_pieces = []
    sums = {}
    for new in rounds:
        places = jnp.stack([jnp.asarray(place, jnp.int32) for place, _, _, _ in new])
        pieces = jnp.stack([piece for _, _, _, piece in new])
        for _, turn, mask, piece in new:
            wide = piece.astype(F32)
            sums[turn, mask] = jnp.sum(wide * wide, axis=1, keepdims=True)
        new_momentum = feedback_columns(
            places, ortho_low, pieces, momentum, gradient, new_momentum
        )
        all_places.append(places)
        all_pieces.append(pieces)
    square_sums = tree_sum([sums[key] for key in sorted(sums)])
    for bit in bits_of("tensor"):
        square_sums = square_sums + swap(square_sums, "tensor", 1 << bit)
    norms = jnp.sqrt(square_sums / all_cols + 1e-06)
    scale = (all_rows / factor.shape[1]) ** 0.5
    step_direction, new_factor = step_outputs(
        jnp.concatenate(all_places), ortho_low, jnp.concatenate(all_pieces), norms, scale
    )
    return (new_momentum, step_direction, new_factor)


def solution(mesh):
    in_specs = (P("dp", "fsdp", "tensor"), P("dp", "fsdp", "tensor"), P("tensor", None))
    out_specs = (P("dp", "fsdp", "tensor"), P("fsdp", "tensor"), P("tensor", None))
    return jax.shard_map(local, mesh=mesh, in_specs=in_specs, out_specs=out_specs, check_vma=False)
```

```python
import functools

import jax
import jax.numpy as jnp
from jax import lax
from jax.experimental import pallas as pl
from jax.experimental.pallas import tpu as pltpu
from jax.sharding import PartitionSpec as P

F32 = jnp.float32
LOW = jnp.bfloat16
LANES = 128
ROOM = 50 << 20
COLS_OVER = (((0,), (0,)), ((), ()))


def inverse_factor_kernel(panel, group, gram_ref, out_ref, work_ref):
    n = gram_ref.shape[0]
    work_ref[...] = jnp.zeros_like(work_ref)
    out_ref[...] = jnp.zeros_like(out_ref)
    rows = lax.broadcasted_iota(jnp.int32, (panel, LANES), 0)
    lanes = lax.broadcasted_iota(jnp.int32, (panel, LANES), 1)
    product = functools.partial(
        lax.dot_general,
        dimension_numbers=COLS_OVER,
        precision=lax.Precision.HIGHEST,
        preferred_element_type=F32,
    )
    for start in range(0, n, panel):
        base = start // LANES * LANES
        wide = base + LANES
        upper = gram_ref[start : start + panel, base:n]
        if start:
            before = work_ref[0:start, start : start + panel]
            upper = upper - product(before, work_ref[0:start, base:n])
            inverse = -product(before, work_ref[0:start, n : n + wide])
            inverse = [inverse[:, c : c + LANES] for c in range(0, wide, LANES)]
        else:
            inverse = [jnp.zeros((panel, LANES), F32)]
        inverse[-1] = inverse[-1] + (lanes == rows + (start - base)).astype(F32)
        upper = [upper[:, c : c + LANES] for c in range(0, n - base, LANES)]
        pivots = jnp.ones((panel, LANES), F32)
        for first in range(0, panel, group):
            lane = start - base + first
            columns = [
                jnp.broadcast_to(upper[0][:, lane + q : lane + q + 1], (panel, LANES))
                for q in range(group)
            ]
            factors = []
            for j in range(group):
                r = first + j
                pivot = columns[j][r : r + 1, :]
                pivots = jnp.where(rows == r, jnp.broadcast_to(pivot, rows.shape), pivots)
                factors.append(jnp.where(rows > r, columns[j] * (1.0 / pivot), 0.0))
                for q in range(j + 1, group):
                    columns[q] = columns[q] - factors[j] * columns[q][r : r + 1, :]
            for j in range(group):
                r = first + j
                upper = [x - factors[j] * x[r : r + 1, :] for x in upper]
                inverse = [x - factors[j] * x[r : r + 1, :] for x in inverse]
        scale = lax.rsqrt(pivots)
        for t, x in enumerate(upper):
            at = base + t * LANES
            work_ref[start : start + panel, at : at + LANES] = x * scale
        for t, x in enumerate(inverse):
            at = t * LANES
            work_ref[start : start + panel, n + at : n + at + LANES] = x * scale
            out_ref[start : start + panel, at : at + LANES] = x * scale


def split_low(x):
    high = x.astype(LOW)
    return high, (x - high.astype(F32)).astype(LOW)


def apply_halves(upper, side_ref, inverse, high_ref, low_ref, out_refs):
    inverse_high, inverse_low = split_low(inverse)
    half = high_ref.shape[1] // 2
    size = half // 2
    width = tile_of(size)
    for turn, out_ref in enumerate(out_refs):
        side = side_ref[turn] if upper else 1 - side_ref[turn]
        for at in range(0, size, width):
            start = pl.multiple_of(side * size + (turn * half + at), LANES)
            high = high_ref[:, pl.ds(start, width)]
            low = low_ref[:, pl.ds(start, width)]
            product = (
                jnp.dot(inverse_high, low, preferred_element_type=F32)
                + jnp.dot(inverse_low, high, preferred_element_type=F32)
            ) + jnp.dot(inverse_high, high, preferred_element_type=F32)
            out_ref[:, at : at + width] = product.astype(out_ref.dtype)


def sent_kernel(side_ref, gram_ref, high_ref, low_ref, inverse_ref, first_ref, second_ref, work_ref):
    inverse_factor_kernel(32, 16, gram_ref, inverse_ref, work_ref)
    apply_halves(False, side_ref, inverse_ref[...], high_ref, low_ref, (first_ref, second_ref))


def kept_kernel(side_ref, inverse_ref, high_ref, low_ref, first_ref, second_ref):
    apply_halves(True, side_ref, inverse_ref[...], high_ref, low_ref, (first_ref, second_ref))


WHOLE = pl.BlockSpec(memory_space=pltpu.VMEM)
SCALARS = pl.BlockSpec(memory_space=pltpu.SMEM)


def inverse_and_sent(side, gram, high, low):
    n, columns = high.shape
    quarter = jax.ShapeDtypeStruct((n, columns // 4), LOW)
    return pl.pallas_call(
        sent_kernel,
        in_specs=[SCALARS, WHOLE, WHOLE, WHOLE],
        out_shape=(jax.ShapeDtypeStruct((n, n), F32), quarter, quarter),
        scratch_shapes=[pltpu.VMEM((n, 2 * n), F32)],
        compiler_params=pltpu.CompilerParams(vmem_limit_bytes=16 << 20),
    )(side, gram, high, low)


def kept_quarters(side, inverse, high, low):
    n, columns = high.shape
    quarter = jax.ShapeDtypeStruct((n, columns // 4), F32)
    return pl.pallas_call(
        kept_kernel,
        in_specs=[SCALARS, WHOLE, WHOLE, WHOLE],
        out_shape=(quarter, quarter),
        compiler_params=pltpu.CompilerParams(vmem_limit_bytes=16 << 20),
    )(side, inverse, high, low)


def tile_of(size):
    return 256 if size % 256 == 0 else LANES


def left_kernel(moment_ref, change_ref, factor_ref, out_ref, low_ref):
    @pl.when(pl.program_id(0) == 0)
    def _():
        low_ref[...] = factor_ref[...].astype(LOW)

    factor = low_ref[...]
    out_ref[...] = jnp.dot(moment_ref[...], factor, preferred_element_type=F32) + jnp.dot(
        change_ref[...], factor, preferred_element_type=F32
    )


def left_product(moment, change, factor):
    rows, columns = moment.shape
    rank = factor.shape[1]
    tile = min(rows, 256)
    return pl.pallas_call(
        left_kernel,
        grid=(rows // tile,),
        in_specs=[
            pl.BlockSpec((tile, columns), lambda i: (i, 0)),
            pl.BlockSpec((tile, columns), lambda i: (i, 0)),
            pl.BlockSpec((columns, rank), lambda i: (0, 0), pipeline_mode=pl.Buffered(1)),
        ],
        out_specs=pl.BlockSpec((tile, rank), lambda i: (i, 0)),
        out_shape=jax.ShapeDtypeStruct((rows, rank), F32),
        scratch_shapes=[pltpu.VMEM((columns, rank), LOW)],
        compiler_params=pltpu.CompilerParams(vmem_limit_bytes=ROOM),
        cost_estimate=pl.CostEstimate(
            flops=4 * rows * columns * rank,
            bytes_accessed=4 * rows * columns,
            transcendentals=0,
        ),
    )(moment, change, factor)


def mixed_product(left_low, moment, change):
    mixed = lax.dot_general(
        left_low, moment, COLS_OVER, preferred_element_type=F32
    ) + lax.dot_general(left_low, change, COLS_OVER, preferred_element_type=F32)
    return split_low(mixed)


def total_kernel(moment_ref, change_ref, first_ref, second_ref):
    rows, columns = moment_ref.shape
    at = pl.multiple_of(pl.program_id(0) * rows, rows)
    total = moment_ref[...].astype(F32) + change_ref[...].astype(F32)
    first_ref[pl.ds(at, rows), :] = total[:, : columns // 2]
    second_ref[pl.ds(at, rows), :] = total[:, columns // 2 :]


def total_of(moment, change):
    rows, columns = moment.shape
    tile = min(rows, 256)
    block = pl.BlockSpec((tile, columns), lambda i: (i, 0))
    return pl.pallas_call(
        total_kernel,
        grid=(rows // tile,),
        in_specs=[block, block],
        out_specs=[WHOLE, WHOLE],
        out_shape=[pltpu.VMEM((rows, columns // 2), F32)] * 2,
        compiler_params=pltpu.CompilerParams(vmem_limit_bytes=12 << 20),
    )(moment, change)


def feedback_kernel(steps, place_ref, ortho_ref, right_ref, first_ref, second_ref, *refs):
    out_ref = refs[-1]
    tile = out_ref.shape[2]
    half = first_ref.shape[1]
    j = pl.program_id(0)
    at = pl.multiple_of((place_ref[j // steps] * steps + j % steps) * tile, tile)
    feedback = jnp.dot(ortho_ref[...], right_ref[0], preferred_element_type=F32)

    @pl.when(at < half)
    def _():
        out_ref[0] = first_ref[:, pl.ds(pl.multiple_of(jnp.minimum(at, half - tile), tile), tile)] - 0.05 * feedback

    @pl.when(at >= half)
    def _():
        out_ref[0] = second_ref[:, pl.ds(pl.multiple_of(jnp.maximum(at - half, 0), tile), tile)] - 0.05 * feedback


def feedback_columns(places, ortho_low, pieces, total, written):
    count, rank, width = pieces.shape
    rows, columns = total[0].shape[0], 2 * total[0].shape[1]
    tile = tile_of(width)
    steps = width // tile

    def column(j, place):
        return (0, 0, place[j // steps] * steps + j % steps)

    specs = [
        pl.BlockSpec((rows, rank), lambda j, place: (0, 0)),
        pl.BlockSpec((1, rank, tile), lambda j, place: (j // steps, 0, j % steps)),
        WHOLE,
        WHOLE,
    ]
    operands = [places, ortho_low, pieces, *total]
    aliases = {}
    if written is not None:
        specs.append(pl.BlockSpec(memory_space=pl.ANY))
        aliases = {len(operands): 0}
        operands.append(written)
    return pl.pallas_call(
        functools.partial(feedback_kernel, steps),
        grid_spec=pltpu.PrefetchScalarGridSpec(
            num_scalar_prefetch=1,
            grid=(count * steps,),
            in_specs=specs,
            out_specs=pl.BlockSpec((1, rows, tile), column),
        ),
        out_shape=jax.ShapeDtypeStruct((1, rows, columns), F32),
        input_output_aliases=aliases,
        compiler_params=pltpu.CompilerParams(vmem_limit_bytes=12 << 20),
    )(*operands)


def step_kernel(scale, place_ref, ortho_ref, right_ref, norm_ref, step_ref, factor_ref):
    factor = right_ref[0].astype(F32) / norm_ref[...]
    product = jnp.dot(ortho_ref[...], factor.astype(LOW), preferred_element_type=F32)
    step_ref[...] = (scale * product).astype(LOW)
    factor_ref[...] = factor.T


def step_outputs(places, ortho_low, pieces, norms, scale):
    count, rank, width = pieces.shape
    rows = ortho_low.shape[0]
    tile = width
    steps = width // tile
    columns = count * width
    return pl.pallas_call(
        functools.partial(step_kernel, scale),
        grid_spec=pltpu.PrefetchScalarGridSpec(
            num_scalar_prefetch=1,
            grid=(count * steps,),
            in_specs=[
                pl.BlockSpec((rows, rank), lambda j, place: (0, 0)),
                pl.BlockSpec((1, rank, tile), lambda j, place: (j // steps, 0, j % steps)),
                pl.BlockSpec((rank, 1), lambda j, place: (0, 0)),
            ],
            out_specs=[
                pl.BlockSpec((rows, tile), lambda j, place: (0, place[j // steps] * steps + j % steps)),
                pl.BlockSpec((tile, rank), lambda j, place: (place[j // steps] * steps + j % steps, 0)),
            ],
        ),
        out_shape=[
            jax.ShapeDtypeStruct((rows, columns), LOW),
            jax.ShapeDtypeStruct((columns, rank), F32),
        ],
        compiler_params=pltpu.CompilerParams(vmem_limit_bytes=16 << 20),
        cost_estimate=pl.CostEstimate(
            flops=2 * rows * rank * columns, bytes_accessed=2 * rows * columns, transcendentals=0
        ),
    )(places, ortho_low, pieces, norms)


def bits_of(axis):
    return range(lax.axis_size(axis).bit_length() - 1)


def swap(x, axis, mask):
    size = lax.axis_size(axis)
    return lax.ppermute(x, axis, [(i, i ^ mask) for i in range(size)])


def halve(x, axis, bit, dtype, dim):
    mine = (lax.axis_index(axis) >> bit) & 1
    size = x.shape[dim] // 2
    kept = lax.dynamic_slice_in_dim(x, mine * size, size, dim)
    sent = lax.dynamic_slice_in_dim(x, (1 - mine) * size, size, dim)
    return kept + swap(sent.astype(dtype), axis, 1 << bit).astype(F32)


def unhalve(x, axis, bit):
    mine = (lax.axis_index(axis) >> bit) & 1
    other = swap(x, axis, 1 << bit)
    return jnp.where(mine == 0, jnp.concatenate([x, other]), jnp.concatenate([other, x]))


def add_both(x, axis, bit):
    low = x.astype(LOW)
    return low.astype(F32) + swap(low, axis, 1 << bit).astype(F32)


def tree_sum(terms):
    while len(terms) > 1:
        terms = [terms[i] + terms[i + 1] for i in range(0, len(terms), 2)]
    return terms[0]


def sum_left(partial):
    for bit in bits_of("tensor"):
        partial = halve(partial, "tensor", bit, F32, 0)
    half = partial.shape[0] // 2
    parts = [partial[:half], partial[half:]]
    bits = list(bits_of("dp"))
    for k in range(len(bits)):
        parts = [
            add_both(part, "dp", bits[(k + turn) % len(bits)]) for turn, part in enumerate(parts)
        ]
    low = (jnp.concatenate(parts) / lax.axis_size("dp")).astype(LOW)
    for bit in reversed(bits_of("tensor")):
        low = unhalve(low, "tensor", bit)
    return low


def sum_gram(gram):
    shards = lax.axis_size("tensor")
    count = gram.shape[0] // shards
    part = lax.dynamic_slice_in_dim(gram, lax.axis_index("tensor") * count, count, 0)
    part = tree_sum([part] + [swap(part, "fsdp", k) for k in range(1, lax.axis_size("fsdp"))])
    for bit in bits_of("tensor"):
        part = unhalve(part, "tensor", bit)
    return part


def orders_of():
    bits = list(bits_of("dp"))
    return [bits[turn % len(bits) :] + bits[: turn % len(bits)] for turn in range(2)]


def scatter_right(gram, high, low):
    orders = orders_of()
    index = lax.axis_index("dp")
    side = jnp.stack([(index >> order[0]) & 1 for order in orders])
    inverse, *sent = inverse_and_sent(side, gram, high, low)
    come = [swap(x, "dp", 1 << order[0]) for x, order in zip(sent, orders)]
    kept = kept_quarters(side, inverse, high, low)
    parts = [a + b.astype(F32) for a, b in zip(kept, come)]
    for k in range(1, len(orders[0])):
        parts = [
            halve(part, "dp", order[k], LOW, 1) for part, order in zip(parts, orders)
        ]
    size = lax.axis_size("fsdp")
    index = lax.axis_index("fsdp")
    width = parts[0].shape[1] // size

    def share(at):
        return jnp.concatenate(
            [lax.dynamic_slice_in_dim(part, at * width, width, 1) for part in parts], axis=1
        )

    terms = [share(index)]
    for k in range(1, size):
        terms.append(swap(share(index ^ k).astype(LOW), "fsdp", k).astype(F32))
    return inverse, tree_sum(terms)


def gather_fsdp(low):
    size = lax.axis_size("fsdp")
    index = lax.axis_index("fsdp")
    width = low.shape[1] // 2
    blocks = [low] + [swap(low, "fsdp", k) for k in range(1, size)]
    for bit in bits_of("fsdp"):
        high = ((index >> bit) & 1) == 1
        blocks = [jnp.where(high, blocks[i ^ (1 << bit)], blocks[i]) for i in range(size)]
    return [
        jnp.concatenate([b[:, :width] for b in blocks], axis=1),
        jnp.concatenate([b[:, width:] for b in blocks], axis=1),
    ]


def gather_rounds(pieces):
    index = lax.axis_index("dp")
    orders = orders_of()
    depth = len(orders[0])
    known = [{0: piece} for piece in pieces]
    rounds = []
    for r in range(depth + 1):
        new = []
        for turn, order in enumerate(orders):
            for mask in range(1 << depth):
                if mask.bit_count() != r:
                    continue
                if r:
                    bit = next(b for b in order if (mask >> b) & 1)
                    known[turn][mask] = swap(known[turn][mask ^ (1 << bit)], "dp", 1 << bit)
                place = turn << depth
                for k, b in enumerate(order):
                    place = place + ((((index ^ mask) >> b) & 1) << (depth - 1 - k))
                new.append((place, turn, mask, known[turn][mask]))
        rounds.append(new)
    return rounds


def local(momentum, gradient, factor):
    replicas = lax.axis_size("dp")
    moment = momentum[0]
    change = gradient[0]
    all_rows = moment.shape[0] * lax.axis_size("fsdp")
    all_cols = moment.shape[1] * lax.axis_size("tensor")
    left_low = sum_left(left_product(moment, change, factor))
    gram = sum_gram(
        lax.dot_general(left_low, left_low, COLS_OVER, preferred_element_type=F32)
    )
    mixed_high, mixed_low = mixed_product(left_low, moment, change)
    inverse, right = scatter_right(gram, mixed_high, mixed_low)
    ortho_low = jnp.dot(
        left_low.astype(F32), inverse.T, precision=lax.Precision.HIGH
    ).astype(LOW)
    moment, change, _ = lax.optimization_barrier((moment, change, inverse))
    total = total_of(moment, change)
    rounds = gather_rounds(gather_fsdp((right / replicas).astype(LOW)))
    new_momentum = None
    all_places = []
    all_pieces = []
    sums = {}
    for new in rounds:
        places = jnp.stack([jnp.asarray(place, jnp.int32) for place, _, _, _ in new])
        pieces = jnp.stack([piece for _, _, _, piece in new])
        for _, turn, mask, piece in new:
            wide = piece.astype(F32)
            sums[turn, mask] = jnp.sum(wide * wide, axis=1, keepdims=True)
        new_momentum = feedback_columns(
            places, ortho_low, pieces, total, new_momentum
        )
        all_places.append(places)
        all_pieces.append(pieces)
    square_sums = tree_sum([sums[key] for key in sorted(sums)])
    for bit in bits_of("tensor"):
        square_sums = square_sums + swap(square_sums, "tensor", 1 << bit)
    norms = jnp.sqrt(square_sums / all_cols + 1e-06)
    scale = (all_rows / factor.shape[1]) ** 0.5
    step_direction, new_factor = step_outputs(
        jnp.concatenate(all_places), ortho_low, jnp.concatenate(all_pieces), norms, scale
    )
    return (new_momentum, step_direction, new_factor)


def solution(mesh):
    in_specs = (P("dp", "fsdp", "tensor"), P("dp", "fsdp", "tensor"), P("tensor", None))
    out_specs = (P("dp", "fsdp", "tensor"), P("fsdp", "tensor"), P("tensor", None))
    return jax.shard_map(local, mesh=mesh, in_specs=in_specs, out_specs=out_specs, check_vma=False)
```

```python
import functools

import jax
import jax.numpy as jnp
from jax import lax
from jax.experimental import pallas as pl
from jax.experimental.pallas import tpu as pltpu
from jax.sharding import PartitionSpec as P

F32 = jnp.float32
LOW = jnp.bfloat16
LANES = 128
ROOM = 50 << 20
COLS_OVER = (((0,), (0,)), ((), ()))


def inverse_factor_kernel(panel, group, gram_ref, out_ref, work_ref):
    n = gram_ref.shape[0]
    work_ref[...] = jnp.zeros_like(work_ref)
    out_ref[...] = jnp.zeros_like(out_ref)
    rows = lax.broadcasted_iota(jnp.int32, (panel, LANES), 0)
    lanes = lax.broadcasted_iota(jnp.int32, (panel, LANES), 1)
    product = functools.partial(
        lax.dot_general,
        dimension_numbers=COLS_OVER,
        precision=lax.Precision.HIGHEST,
        preferred_element_type=F32,
    )
    for start in range(0, n, panel):
        base = start // LANES * LANES
        wide = base + LANES
        upper = gram_ref[start : start + panel, base:n]
        if start:
            before = work_ref[0:start, start : start + panel]
            upper = upper - product(before, work_ref[0:start, base:n])
            inverse = -product(before, work_ref[0:start, n : n + wide])
            inverse = [inverse[:, c : c + LANES] for c in range(0, wide, LANES)]
        else:
            inverse = [jnp.zeros((panel, LANES), F32)]
        inverse[-1] = inverse[-1] + (lanes == rows + (start - base)).astype(F32)
        upper = [upper[:, c : c + LANES] for c in range(0, n - base, LANES)]
        pivots = jnp.ones((panel, LANES), F32)
        for first in range(0, panel, group):
            lane = start - base + first
            columns = [
                jnp.broadcast_to(upper[0][:, lane + q : lane + q + 1], (panel, LANES))
                for q in range(group)
            ]
            factors = []
            for j in range(group):
                r = first + j
                pivot = columns[j][r : r + 1, :]
                pivots = jnp.where(rows == r, jnp.broadcast_to(pivot, rows.shape), pivots)
                factors.append(jnp.where(rows > r, columns[j] * (1.0 / pivot), 0.0))
                for q in range(j + 1, group):
                    columns[q] = columns[q] - factors[j] * columns[q][r : r + 1, :]
            for j in range(group):
                r = first + j
                upper = [x - factors[j] * x[r : r + 1, :] for x in upper]
                inverse = [x - factors[j] * x[r : r + 1, :] for x in inverse]
        scale = lax.rsqrt(pivots)
        for t, x in enumerate(upper):
            at = base + t * LANES
            work_ref[start : start + panel, at : at + LANES] = x * scale
        for t, x in enumerate(inverse):
            at = t * LANES
            work_ref[start : start + panel, n + at : n + at + LANES] = x * scale
            out_ref[start : start + panel, at : at + LANES] = x * scale


def split_low(x):
    high = x.astype(LOW)
    return high, (x - high.astype(F32)).astype(LOW)


def apply_halves(upper, side_ref, inverse, mixed_ref, out_refs):
    inverse_high, inverse_low = split_low(inverse)
    half = mixed_ref.shape[1] // 2
    size = half // 2
    width = tile_of(size)
    for turn, out_ref in enumerate(out_refs):
        side = side_ref[turn] if upper else 1 - side_ref[turn]
        for at in range(0, size, width):
            start = pl.multiple_of(side * size + (turn * half + at), LANES)
            high, low = split_low(mixed_ref[:, pl.ds(start, width)])
            product = (
                jnp.dot(inverse_high, low, preferred_element_type=F32)
                + jnp.dot(inverse_low, high, preferred_element_type=F32)
            ) + jnp.dot(inverse_high, high, preferred_element_type=F32)
            out_ref[:, at : at + width] = product.astype(out_ref.dtype)


def sent_kernel(side_ref, gram_ref, mixed_ref, inverse_ref, first_ref, second_ref, work_ref):
    inverse_factor_kernel(32, 16, gram_ref, inverse_ref, work_ref)
    apply_halves(False, side_ref, inverse_ref[...], mixed_ref, (first_ref, second_ref))


def kept_kernel(side_ref, inverse_ref, mixed_ref, first_ref, second_ref):
    apply_halves(True, side_ref, inverse_ref[...], mixed_ref, (first_ref, second_ref))


WHOLE = pl.BlockSpec(memory_space=pltpu.VMEM)
SCALARS = pl.BlockSpec(memory_space=pltpu.SMEM)


def inverse_and_sent(side, gram, mixed):
    n, columns = mixed.shape
    quarter = jax.ShapeDtypeStruct((n, columns // 4), LOW)
    return pl.pallas_call(
        sent_kernel,
        in_specs=[SCALARS, WHOLE, WHOLE],
        out_shape=(jax.ShapeDtypeStruct((n, n), F32), quarter, quarter),
        scratch_shapes=[pltpu.VMEM((n, 2 * n), F32)],
        compiler_params=pltpu.CompilerParams(vmem_limit_bytes=16 << 20),
    )(side, gram, mixed)


def kept_quarters(side, inverse, mixed):
    n, columns = mixed.shape
    quarter = jax.ShapeDtypeStruct((n, columns // 4), F32)
    return pl.pallas_call(
        kept_kernel,
        in_specs=[SCALARS, WHOLE, WHOLE],
        out_shape=(quarter, quarter),
        compiler_params=pltpu.CompilerParams(vmem_limit_bytes=16 << 20),
    )(side, inverse, mixed)


def tile_of(size):
    return 256 if size % 256 == 0 else LANES


def left_kernel(moment_ref, change_ref, factor_ref, out_ref, low_ref):
    @pl.when(pl.program_id(0) == 0)
    def _():
        low_ref[...] = factor_ref[...].astype(LOW)

    factor = low_ref[...]
    out_ref[...] = jnp.dot(moment_ref[...], factor, preferred_element_type=F32) + jnp.dot(
        change_ref[...], factor, preferred_element_type=F32
    )


def left_product(moment, change, factor):
    rows, columns = moment.shape
    rank = factor.shape[1]
    tile = min(rows, 512)
    return pl.pallas_call(
        left_kernel,
        grid=(rows // tile,),
        in_specs=[
            pl.BlockSpec((tile, columns), lambda i: (i, 0)),
            pl.BlockSpec((tile, columns), lambda i: (i, 0)),
            pl.BlockSpec((columns, rank), lambda i: (0, 0), pipeline_mode=pl.Buffered(1)),
        ],
        out_specs=pl.BlockSpec((tile, rank), lambda i: (i, 0)),
        out_shape=jax.ShapeDtypeStruct((rows, rank), F32),
        scratch_shapes=[pltpu.VMEM((columns, rank), LOW)],
        compiler_params=pltpu.CompilerParams(vmem_limit_bytes=ROOM),
        cost_estimate=pl.CostEstimate(
            flops=4 * rows * columns * rank,
            bytes_accessed=4 * rows * columns,
            transcendentals=0,
        ),
    )(moment, change, factor)


def mixed_product(left_low, moment, change):
    return lax.dot_general(
        left_low, moment, COLS_OVER, preferred_element_type=F32
    ) + lax.dot_general(left_low, change, COLS_OVER, preferred_element_type=F32)


def total_kernel(moment_ref, change_ref, first_ref, second_ref):
    rows, columns = moment_ref.shape
    at = pl.multiple_of(pl.program_id(0) * rows, rows)
    total = moment_ref[...].astype(F32) + change_ref[...].astype(F32)
    first_ref[pl.ds(at, rows), :] = total[:, : columns // 2]
    second_ref[pl.ds(at, rows), :] = total[:, columns // 2 :]


def total_of(moment, change):
    rows, columns = moment.shape
    tile = min(rows, 256)
    block = pl.BlockSpec((tile, columns), lambda i: (i, 0))
    return pl.pallas_call(
        total_kernel,
        grid=(rows // tile,),
        in_specs=[block, block],
        out_specs=[WHOLE, WHOLE],
        out_shape=[pltpu.VMEM((rows, columns // 2), F32)] * 2,
        compiler_params=pltpu.CompilerParams(vmem_limit_bytes=12 << 20),
    )(moment, change)


def feedback_kernel(steps, place_ref, ortho_ref, right_ref, first_ref, second_ref, *refs):
    out_ref = refs[-1]
    tile = out_ref.shape[2]
    half = first_ref.shape[1]
    j = pl.program_id(0)
    at = pl.multiple_of((place_ref[j // steps] * steps + j % steps) * tile, tile)
    feedback = jnp.dot(ortho_ref[...], right_ref[0], preferred_element_type=F32)

    @pl.when(at < half)
    def _():
        out_ref[0] = first_ref[:, pl.ds(pl.multiple_of(jnp.minimum(at, half - tile), tile), tile)] - 0.05 * feedback

    @pl.when(at >= half)
    def _():
        out_ref[0] = second_ref[:, pl.ds(pl.multiple_of(jnp.maximum(at - half, 0), tile), tile)] - 0.05 * feedback


def feedback_columns(places, ortho_low, pieces, total, written):
    count, rank, width = pieces.shape
    rows, columns = total[0].shape[0], 2 * total[0].shape[1]
    tile = width
    steps = width // tile

    def column(j, place):
        return (0, 0, place[j // steps] * steps + j % steps)

    specs = [
        WHOLE,
        pl.BlockSpec((1, rank, tile), lambda j, place: (j // steps, 0, j % steps)),
        WHOLE,
        WHOLE,
    ]
    operands = [places, ortho_low, pieces, *total]
    aliases = {}
    if written is not None:
        specs.append(pl.BlockSpec(memory_space=pl.ANY))
        aliases = {len(operands): 0}
        operands.append(written)
    return pl.pallas_call(
        functools.partial(feedback_kernel, steps),
        grid_spec=pltpu.PrefetchScalarGridSpec(
            num_scalar_prefetch=1,
            grid=(count * steps,),
            in_specs=specs,
            out_specs=pl.BlockSpec((1, rows, tile), column),
        ),
        out_shape=jax.ShapeDtypeStruct((1, rows, columns), F32),
        input_output_aliases=aliases,
        compiler_params=pltpu.CompilerParams(vmem_limit_bytes=12 << 20),
    )(*operands)


def step_kernel(scale, counts, place_ref, ortho_ref, *refs):
    norm_ref, step_ref, factor_ref, work_ref = refs[len(counts) :]
    j = pl.program_id(0)
    first = 0
    for count, right_ref in zip(counts, refs):
        for at in range(count):

            @pl.when(j == first + at)
            def _():
                work_ref[...] = right_ref[at].astype(F32) / norm_ref[...]

        first += count
    factor = work_ref[...]
    product = jnp.dot(ortho_ref[...], factor.astype(LOW), preferred_element_type=F32)
    step_ref[...] = (scale * product).astype(LOW)
    factor_ref[...] = factor.T


def step_outputs(places, ortho_low, rounds, norms, scale):
    counts = [pieces.shape[0] for pieces in rounds]
    _, rank, width = rounds[0].shape
    rows = ortho_low.shape[0]
    columns = sum(counts) * width
    return pl.pallas_call(
        functools.partial(step_kernel, scale, counts),
        grid_spec=pltpu.PrefetchScalarGridSpec(
            num_scalar_prefetch=1,
            grid=(sum(counts),),
            in_specs=[pl.BlockSpec((rows, rank), lambda j, place: (0, 0))]
            + [WHOLE] * len(counts)
            + [pl.BlockSpec((rank, 1), lambda j, place: (0, 0))],
            out_specs=[
                pl.BlockSpec((rows, width), lambda j, place: (0, place[j])),
                pl.BlockSpec((width, rank), lambda j, place: (place[j], 0)),
            ],
            scratch_shapes=[pltpu.VMEM((rank, width), F32)],
        ),
        out_shape=[
            jax.ShapeDtypeStruct((rows, columns), LOW),
            jax.ShapeDtypeStruct((columns, rank), F32),
        ],
        compiler_params=pltpu.CompilerParams(vmem_limit_bytes=16 << 20),
    )(places, ortho_low, *rounds, norms)


def bits_of(axis):
    return range(lax.axis_size(axis).bit_length() - 1)


def swap(x, axis, mask):
    size = lax.axis_size(axis)
    return lax.ppermute(x, axis, [(i, i ^ mask) for i in range(size)])


def halve(x, axis, bit, dtype, dim):
    mine = (lax.axis_index(axis) >> bit) & 1
    size = x.shape[dim] // 2
    kept = lax.dynamic_slice_in_dim(x, mine * size, size, dim)
    sent = lax.dynamic_slice_in_dim(x, (1 - mine) * size, size, dim)
    return kept + swap(sent.astype(dtype), axis, 1 << bit).astype(F32)


def unhalve(x, axis, bit):
    mine = (lax.axis_index(axis) >> bit) & 1
    other = swap(x, axis, 1 << bit)
    return jnp.where(mine == 0, jnp.concatenate([x, other]), jnp.concatenate([other, x]))


def add_both(x, axis, bit):
    low = x.astype(LOW)
    return low.astype(F32) + swap(low, axis, 1 << bit).astype(F32)


def tree_sum(terms):
    while len(terms) > 1:
        terms = [terms[i] + terms[i + 1] for i in range(0, len(terms), 2)]
    return terms[0]


def sum_left(partial):
    for bit in bits_of("tensor"):
        partial = halve(partial, "tensor", bit, F32, 0)
    half = partial.shape[0] // 2
    parts = [partial[:half], partial[half:]]
    bits = list(bits_of("dp"))
    for k in range(len(bits)):
        parts = [
            add_both(part, "dp", bits[(k + turn) % len(bits)]) for turn, part in enumerate(parts)
        ]
    low = (jnp.concatenate(parts) / lax.axis_size("dp")).astype(LOW)
    for bit in reversed(bits_of("tensor")):
        low = unhalve(low, "tensor", bit)
    return low


def sum_gram(gram):
    shards = lax.axis_size("tensor")
    count = gram.shape[0] // shards
    part = lax.dynamic_slice_in_dim(gram, lax.axis_index("tensor") * count, count, 0)
    part = tree_sum([part] + [swap(part, "fsdp", k) for k in range(1, lax.axis_size("fsdp"))])
    for bit in bits_of("tensor"):
        part = unhalve(part, "tensor", bit)
    return part


def orders_of():
    bits = list(bits_of("dp"))
    return [bits[turn % len(bits) :] + bits[: turn % len(bits)] for turn in range(2)]


def scatter_right(gram, mixed):
    orders = orders_of()
    index = lax.axis_index("dp")
    side = jnp.stack([(index >> order[0]) & 1 for order in orders])
    inverse, *sent = inverse_and_sent(side, gram, mixed)
    come = [swap(x, "dp", 1 << order[0]) for x, order in zip(sent, orders)]
    kept = kept_quarters(side, inverse, mixed)
    parts = [a + b.astype(F32) for a, b in zip(kept, come)]
    for k in range(1, len(orders[0])):
        parts = [
            halve(part, "dp", order[k], LOW, 1) for part, order in zip(parts, orders)
        ]
    size = lax.axis_size("fsdp")
    index = lax.axis_index("fsdp")
    width = parts[0].shape[1] // size

    def share(at):
        return jnp.concatenate(
            [lax.dynamic_slice_in_dim(part, at * width, width, 1) for part in parts], axis=1
        )

    terms = [share(index)]
    for k in range(1, size):
        terms.append(swap(share(index ^ k).astype(LOW), "fsdp", k).astype(F32))
    return inverse, tree_sum(terms)


def gather_fsdp(low):
    size = lax.axis_size("fsdp")
    index = lax.axis_index("fsdp")
    width = low.shape[1] // 2
    blocks = [low] + [swap(low, "fsdp", k) for k in range(1, size)]
    for bit in bits_of("fsdp"):
        high = ((index >> bit) & 1) == 1
        blocks = [jnp.where(high, blocks[i ^ (1 << bit)], blocks[i]) for i in range(size)]
    return [
        jnp.concatenate([b[:, :width] for b in blocks], axis=1),
        jnp.concatenate([b[:, width:] for b in blocks], axis=1),
    ]


def gather_rounds(pieces):
    index = lax.axis_index("dp")
    orders = orders_of()
    depth = len(orders[0])
    known = [{0: piece} for piece in pieces]
    rounds = []
    for r in range(depth + 1):
        new = []
        for turn, order in enumerate(orders):
            for mask in range(1 << depth):
                if mask.bit_count() != r:
                    continue
                if r:
                    bit = next(b for b in order if (mask >> b) & 1)
                    known[turn][mask] = swap(known[turn][mask ^ (1 << bit)], "dp", 1 << bit)
                place = turn << depth
                for k, b in enumerate(order):
                    place = place + ((((index ^ mask) >> b) & 1) << (depth - 1 - k))
                new.append((place, turn, mask, known[turn][mask]))
        rounds.append(new)
    return rounds


def local(momentum, gradient, factor):
    replicas = lax.axis_size("dp")
    moment = momentum[0]
    change = gradient[0]
    all_rows = moment.shape[0] * lax.axis_size("fsdp")
    all_cols = moment.shape[1] * lax.axis_size("tensor")
    left_low = sum_left(left_product(moment, change, factor))
    gram = sum_gram(
        lax.dot_general(left_low, left_low, COLS_OVER, preferred_element_type=F32)
    )
    mixed = mixed_product(left_low, moment, change)
    inverse, right = scatter_right(gram, mixed)
    ortho_low = jnp.dot(
        left_low.astype(F32), inverse.T, precision=lax.Precision.HIGH
    ).astype(LOW)
    moment, change, _ = lax.optimization_barrier((moment, change, inverse))
    total = total_of(moment, change)
    rounds = gather_rounds(gather_fsdp((right / replicas).astype(LOW)))
    new_momentum = None
    all_places = []
    all_pieces = []
    sums = {}
    for new in rounds:
        places = jnp.stack([jnp.asarray(place, jnp.int32) for place, _, _, _ in new])
        pieces = jnp.stack([piece for _, _, _, piece in new])
        for _, turn, mask, piece in new:
            wide = piece.astype(F32)
            sums[turn, mask] = jnp.sum(wide * wide, axis=1, keepdims=True)
        new_momentum = feedback_columns(
            places, ortho_low, pieces, total, new_momentum
        )
        all_places.append(places)
        all_pieces.append(pieces)
    square_sums = tree_sum([sums[key] for key in sorted(sums)])
    for bit in bits_of("tensor"):
        square_sums = square_sums + swap(square_sums, "tensor", 1 << bit)
    norms = jnp.sqrt(square_sums / all_cols + 1e-06)
    scale = (all_rows / factor.shape[1]) ** 0.5
    step_direction, new_factor = step_outputs(
        jnp.concatenate(all_places), ortho_low, all_pieces, norms, scale
    )
    return (new_momentum, step_direction, new_factor)


def solution(mesh):
    in_specs = (P("dp", "fsdp", "tensor"), P("dp", "fsdp", "tensor"), P("tensor", None))
    out_specs = (P("dp", "fsdp", "tensor"), P("fsdp", "tensor"), P("tensor", None))
    return jax.shard_map(local, mesh=mesh, in_specs=in_specs, out_specs=out_specs, check_vma=False)
```

```python
import functools

import jax
import jax.numpy as jnp
from jax import lax
from jax.experimental import pallas as pl
from jax.experimental.pallas import tpu as pltpu
from jax.sharding import PartitionSpec as P

F32 = jnp.float32
LOW = jnp.bfloat16
LANES = 128
ROOM = 50 << 20
COLS_OVER = (((0,), (0,)), ((), ()))


def inverse_factor_kernel(panel, group, gram_ref, out_ref, work_ref):
    n = gram_ref.shape[0]
    work_ref[...] = jnp.zeros_like(work_ref)
    out_ref[...] = jnp.zeros_like(out_ref)
    rows = lax.broadcasted_iota(jnp.int32, (panel, LANES), 0)
    lanes = lax.broadcasted_iota(jnp.int32, (panel, LANES), 1)
    product = functools.partial(
        lax.dot_general,
        dimension_numbers=COLS_OVER,
        precision=lax.Precision.HIGHEST,
        preferred_element_type=F32,
    )
    for start in range(0, n, panel):
        base = start // LANES * LANES
        wide = base + LANES
        upper = gram_ref[start : start + panel, base:n]
        if start:
            before = work_ref[0:start, start : start + panel]
            upper = upper - product(before, work_ref[0:start, base:n])
            inverse = -product(before, work_ref[0:start, n : n + wide])
            inverse = [inverse[:, c : c + LANES] for c in range(0, wide, LANES)]
        else:
            inverse = [jnp.zeros((panel, LANES), F32)]
        inverse[-1] = inverse[-1] + (lanes == rows + (start - base)).astype(F32)
        upper = [upper[:, c : c + LANES] for c in range(0, n - base, LANES)]
        pivots = jnp.ones((panel, LANES), F32)
        for first in range(0, panel, group):
            lane = start - base + first
            columns = [
                jnp.broadcast_to(upper[0][:, lane + q : lane + q + 1], (panel, LANES))
                for q in range(group)
            ]
            factors = []
            for j in range(group):
                r = first + j
                pivot = columns[j][r : r + 1, :]
                pivots = jnp.where(rows == r, jnp.broadcast_to(pivot, rows.shape), pivots)
                factors.append(jnp.where(rows > r, columns[j] * (1.0 / pivot), 0.0))
                for q in range(j + 1, group):
                    columns[q] = columns[q] - factors[j] * columns[q][r : r + 1, :]
            for j in range(group):
                r = first + j
                upper = [x - factors[j] * x[r : r + 1, :] for x in upper]
                inverse = [x - factors[j] * x[r : r + 1, :] for x in inverse]
        scale = lax.rsqrt(pivots)
        for t, x in enumerate(upper):
            at = base + t * LANES
            work_ref[start : start + panel, at : at + LANES] = x * scale
        for t, x in enumerate(inverse):
            at = t * LANES
            work_ref[start : start + panel, n + at : n + at + LANES] = x * scale
            out_ref[start : start + panel, at : at + LANES] = x * scale


def split_low(x):
    high = x.astype(LOW)
    return high, (x - high.astype(F32)).astype(LOW)


def apply_inverse(inverse, mixed):
    inverse_high, inverse_low = split_low(inverse)
    high, low = split_low(mixed)
    return (
        jnp.dot(inverse_high, low, preferred_element_type=F32)
        + jnp.dot(inverse_low, high, preferred_element_type=F32)
    ) + jnp.dot(inverse_high, high, preferred_element_type=F32)


def sent_kernel(gram_ref, mixed_ref, inverse_ref, first_ref, second_ref, work_ref):
    inverse_factor_kernel(32, 16, gram_ref, inverse_ref, work_ref)
    inverse = inverse_ref[...]
    size = first_ref.shape[1]
    width = tile_of(size)
    for turn, out_ref in enumerate((first_ref, second_ref)):
        for at in range(0, size, width):
            mixed = mixed_ref[:, turn * size + at : turn * size + at + width]
            out_ref[:, at : at + width] = apply_inverse(inverse, mixed).astype(LOW)


def mixed_of(left_ref, moment_ref, change_ref):
    left = left_ref[...]
    return jnp.dot(left, moment_ref[...], preferred_element_type=F32) + jnp.dot(
        left, change_ref[...], preferred_element_type=F32
    )


def mixed_kernel(side_ref, left_ref, moment_ref, change_ref, out_ref):
    out_ref[...] = mixed_of(left_ref, moment_ref, change_ref)


def kept_kernel(side_ref, left_ref, moment_ref, change_ref, inverse_ref, out_ref):
    mixed = mixed_of(left_ref, moment_ref, change_ref)
    out_ref[...] = apply_inverse(inverse_ref[...], mixed)


WHOLE = pl.BlockSpec(memory_space=pltpu.VMEM)


def quarters_product(body, side, left_turned, moment, change, *operands):
    rank, rows = left_turned.shape
    columns = moment.shape[1]
    tile = min(columns // 4, 512)
    steps = columns // 4 // tile

    def place(j, side):
        return (0, (2 * (j // steps) + side[j // steps]) * steps + j % steps)

    block = pl.BlockSpec((rows, tile), place)
    return pl.pallas_call(
        body,
        grid_spec=pltpu.PrefetchScalarGridSpec(
            num_scalar_prefetch=1,
            grid=(2 * steps,),
            in_specs=[pl.BlockSpec((rank, rows), lambda j, side: (0, 0)), block, block]
            + [WHOLE] * len(operands),
            out_specs=pl.BlockSpec((rank, tile), lambda j, side: (0, j)),
        ),
        out_shape=jax.ShapeDtypeStruct((rank, columns // 2), F32),
        compiler_params=pltpu.CompilerParams(vmem_limit_bytes=ROOM),
    )(side, left_turned, moment, change, *operands)


def inverse_and_sent(gram, mixed):
    n, columns = mixed.shape
    quarter = jax.ShapeDtypeStruct((n, columns // 2), LOW)
    return pl.pallas_call(
        sent_kernel,
        out_shape=(jax.ShapeDtypeStruct((n, n), F32), quarter, quarter),
        scratch_shapes=[pltpu.VMEM((n, 2 * n), F32)],
        compiler_params=pltpu.CompilerParams(vmem_limit_bytes=16 << 20),
    )(gram, mixed)


def tile_of(size):
    return 256 if size % 256 == 0 else LANES


def left_kernel(moment_ref, change_ref, factor_ref, out_ref, low_ref):
    @pl.when(pl.program_id(0) == 0)
    def _():
        low_ref[...] = factor_ref[...].astype(LOW)

    factor = low_ref[...]
    out_ref[...] = jnp.dot(moment_ref[...], factor, preferred_element_type=F32) + jnp.dot(
        change_ref[...], factor, preferred_element_type=F32
    )


def left_product(moment, change, factor):
    rows, columns = moment.shape
    rank = factor.shape[1]
    tile = min(rows, 512)
    return pl.pallas_call(
        left_kernel,
        grid=(rows // tile,),
        in_specs=[
            pl.BlockSpec((tile, columns), lambda i: (i, 0)),
            pl.BlockSpec((tile, columns), lambda i: (i, 0)),
            pl.BlockSpec((columns, rank), lambda i: (0, 0), pipeline_mode=pl.Buffered(1)),
        ],
        out_specs=pl.BlockSpec((tile, rank), lambda i: (i, 0)),
        out_shape=jax.ShapeDtypeStruct((rows, rank), F32),
        scratch_shapes=[pltpu.VMEM((columns, rank), LOW)],
        compiler_params=pltpu.CompilerParams(vmem_limit_bytes=ROOM),
        cost_estimate=pl.CostEstimate(
            flops=4 * rows * columns * rank,
            bytes_accessed=4 * rows * columns,
            transcendentals=0,
        ),
    )(moment, change, factor)


def total_kernel(counts, place_ref, moment_ref, change_ref, *out_refs):
    j = pl.program_id(0)
    width = moment_ref.shape[1]
    first = 0
    for count, out_ref in zip(counts, out_refs):

        @pl.when((j >= first) & (j < first + count))
        def _():
            at = jnp.clip(j - first, 0, count - 1) * width
            out_ref[:, pl.ds(pl.multiple_of(at, width), width)] = moment_ref[...].astype(
                F32
            ) + change_ref[...].astype(F32)

        first += count


def totals_of(places, width, moment, change):
    rows = moment.shape[0]
    counts = [place.shape[0] for place in places]
    block = pl.BlockSpec((rows, width), lambda j, place: (0, place[j]))
    return pl.pallas_call(
        functools.partial(total_kernel, counts),
        grid_spec=pltpu.PrefetchScalarGridSpec(
            num_scalar_prefetch=1,
            grid=(sum(counts),),
            in_specs=[block, block],
            out_specs=[WHOLE] * len(counts),
        ),
        out_shape=[pltpu.VMEM((rows, count * width), F32) for count in counts],
        compiler_params=pltpu.CompilerParams(vmem_limit_bytes=14 << 20),
    )(jnp.concatenate(places), moment, change)


def first_kernel(place_ref, ortho_ref, right_ref, moment_ref, change_ref, out_ref):
    feedback = jnp.dot(ortho_ref[...], right_ref[0], preferred_element_type=F32)
    out_ref[0] = moment_ref[...].astype(F32) + change_ref[...].astype(F32) - 0.05 * feedback


def later_kernel(place_ref, ortho_ref, right_ref, total_ref, written_ref, out_ref):
    width = out_ref.shape[2]
    at = pl.multiple_of(pl.program_id(0) * width, width)
    feedback = jnp.dot(ortho_ref[...], right_ref[0], preferred_element_type=F32)
    out_ref[0] = total_ref[:, pl.ds(at, width)] - 0.05 * feedback


def feedback_columns(places, ortho_low, pieces, moment, change, total, written):
    count, rank, width = pieces.shape
    rows, columns = moment.shape
    specs = [WHOLE, pl.BlockSpec((1, rank, width), lambda j, place: (j, 0, 0))]
    if written is None:
        tile = tile_of(width)
        steps = width // tile
        specs[1] = pl.BlockSpec((1, rank, tile), lambda j, place: (j // steps, 0, j % steps))
        block = pl.BlockSpec(
            (rows, tile), lambda j, place: (0, place[j // steps] * steps + j % steps)
        )
        specs += [block, block]
        operands = [moment, change]
        aliases = {}
    else:
        tile, steps = width, 1
        specs += [WHOLE, pl.BlockSpec(memory_space=pl.ANY)]
        operands = [total, written]
        aliases = {4: 0}
    return pl.pallas_call(
        first_kernel if written is None else later_kernel,
        grid_spec=pltpu.PrefetchScalarGridSpec(
            num_scalar_prefetch=1,
            grid=(count * steps,),
            in_specs=specs,
            out_specs=pl.BlockSpec(
                (1, rows, tile), lambda j, place: (0, 0, place[j // steps] * steps + j % steps)
            ),
        ),
        out_shape=jax.ShapeDtypeStruct((1, rows, columns), F32),
        input_output_aliases=aliases,
        compiler_params=pltpu.CompilerParams(vmem_limit_bytes=12 << 20),
    )(places, ortho_low, pieces, *operands)


def step_kernel(scale, starts, place_ref, ortho_ref, *refs):
    norm_ref, step_ref, factor_ref, work_ref = refs[len(starts) :]
    j = pl.program_id(0)
    for start, right_ref in zip(starts, refs):

        @pl.when(j >= start)
        def _():
            work_ref[...] = right_ref[0].astype(F32) / norm_ref[...]

    factor = work_ref[...]
    product = jnp.dot(ortho_ref[...], factor.astype(LOW), preferred_element_type=F32)
    step_ref[...] = (scale * product).astype(LOW)
    factor_ref[...] = factor.T


def step_outputs(places, ortho_low, rounds, norms, scale):
    counts = [pieces.shape[0] for pieces in rounds]
    starts = [sum(counts[:r]) for r in range(len(counts))]
    _, rank, width = rounds[0].shape
    rows = ortho_low.shape[0]
    columns = sum(counts) * width

    def piece_block(start, count):
        return pl.BlockSpec(
            (1, rank, width), lambda j, place: (jnp.clip(j - start, 0, count - 1), 0, 0)
        )

    return pl.pallas_call(
        functools.partial(step_kernel, scale, starts),
        grid_spec=pltpu.PrefetchScalarGridSpec(
            num_scalar_prefetch=1,
            grid=(sum(counts),),
            in_specs=[pl.BlockSpec((rows, rank), lambda j, place: (0, 0))]
            + [piece_block(start, count) for start, count in zip(starts, counts)]
            + [pl.BlockSpec((rank, 1), lambda j, place: (0, 0))],
            out_specs=[
                pl.BlockSpec((rows, width), lambda j, place: (0, place[j])),
                pl.BlockSpec((width, rank), lambda j, place: (place[j], 0)),
            ],
            scratch_shapes=[pltpu.VMEM((rank, width), F32)],
        ),
        out_shape=[
            jax.ShapeDtypeStruct((rows, columns), LOW),
            jax.ShapeDtypeStruct((columns, rank), F32),
        ],
        compiler_params=pltpu.CompilerParams(vmem_limit_bytes=16 << 20),
    )(
        places,
        ortho_low,
        *(pltpu.with_memory_space_constraint(pieces, pltpu.HBM) for pieces in rounds),
        norms,
    )


def bits_of(axis):
    return range(lax.axis_size(axis).bit_length() - 1)


def swap(x, axis, mask):
    size = lax.axis_size(axis)
    return lax.ppermute(x, axis, [(i, i ^ mask) for i in range(size)])


def halve(x, axis, bit, dtype, dim):
    mine = (lax.axis_index(axis) >> bit) & 1
    size = x.shape[dim] // 2
    kept = lax.dynamic_slice_in_dim(x, mine * size, size, dim)
    sent = lax.dynamic_slice_in_dim(x, (1 - mine) * size, size, dim)
    return kept + swap(sent.astype(dtype), axis, 1 << bit).astype(F32)


def unhalve(x, axis, bit):
    mine = (lax.axis_index(axis) >> bit) & 1
    other = swap(x, axis, 1 << bit)
    return jnp.where(mine == 0, jnp.concatenate([x, other]), jnp.concatenate([other, x]))


def add_both(x, axis, bit):
    low = x.astype(LOW)
    return low.astype(F32) + swap(low, axis, 1 << bit).astype(F32)


def tree_sum(terms):
    while len(terms) > 1:
        terms = [terms[i] + terms[i + 1] for i in range(0, len(terms), 2)]
    return terms[0]


def sum_left(partial):
    for bit in bits_of("tensor"):
        partial = halve(partial, "tensor", bit, F32, 0)
    half = partial.shape[0] // 2
    parts = [partial[:half], partial[half:]]
    bits = list(bits_of("dp"))
    for k in range(len(bits)):
        parts = [
            add_both(part, "dp", bits[(k + turn) % len(bits)]) for turn, part in enumerate(parts)
        ]
    low = (jnp.concatenate(parts) / lax.axis_size("dp")).astype(LOW)
    for bit in reversed(bits_of("tensor")):
        low = unhalve(low, "tensor", bit)
    return low


def sum_gram(gram, mixed):
    shards = lax.axis_size("tensor")
    count = gram.shape[0] // shards
    part = lax.dynamic_slice_in_dim(gram, lax.axis_index("tensor") * count, count, 0)
    part = tree_sum([part] + [swap(part, "fsdp", k) for k in range(1, lax.axis_size("fsdp"))])
    part, mixed = lax.optimization_barrier((part, mixed))
    for bit in bits_of("tensor"):
        part = unhalve(part, "tensor", bit)
    return part, mixed


def orders_of():
    bits = list(bits_of("dp"))
    return [bits[turn % len(bits) :] + bits[: turn % len(bits)] for turn in range(2)]


def sides_of():
    index = lax.axis_index("dp")
    return jnp.stack([(index >> order[0]) & 1 for order in orders_of()])


def scatter_right(sent, keep):
    orders = orders_of()
    come = [swap(x, "dp", 1 << order[0]) for x, order in zip(sent, orders)]
    kept = keep()
    size = kept.shape[1] // 2
    parts = [a + b.astype(F32) for a, b in zip((kept[:, :size], kept[:, size:]), come)]
    for k in range(1, len(orders[0])):
        parts = [
            halve(part, "dp", order[k], LOW, 1) for part, order in zip(parts, orders)
        ]
    size = lax.axis_size("fsdp")
    index = lax.axis_index("fsdp")
    width = parts[0].shape[1] // size

    def share(at):
        return jnp.concatenate(
            [lax.dynamic_slice_in_dim(part, at * width, width, 1) for part in parts], axis=1
        )

    terms = [share(index)]
    for k in range(1, size):
        terms.append(swap(share(index ^ k).astype(LOW), "fsdp", k).astype(F32))
    return tree_sum(terms)


def gather_fsdp(low):
    size = lax.axis_size("fsdp")
    index = lax.axis_index("fsdp")
    width = low.shape[1] // 2
    blocks = [low] + [swap(low, "fsdp", k) for k in range(1, size)]
    for bit in bits_of("fsdp"):
        high = ((index >> bit) & 1) == 1
        blocks = [jnp.where(high, blocks[i ^ (1 << bit)], blocks[i]) for i in range(size)]
    return [
        jnp.concatenate([b[:, :width] for b in blocks], axis=1),
        jnp.concatenate([b[:, width:] for b in blocks], axis=1),
    ]


def masks_of():
    depth = len(orders_of()[0])
    return [
        [(turn, mask) for turn in range(2) for mask in range(1 << depth) if mask.bit_count() == r]
        for r in range(depth + 1)
    ]


def places_of(masks):
    index = lax.axis_index("dp")
    orders = orders_of()
    depth = len(orders[0])
    places = []
    for turn, mask in masks:
        place = jnp.int32(turn << depth)
        for k, b in enumerate(orders[turn]):
            place = place + ((((index ^ mask) >> b) & 1) << (depth - 1 - k))
        places.append(place)
    return jnp.stack(places)


def gather_rounds(pieces):
    known = {(turn, 0): piece for turn, piece in enumerate(pieces)}
    orders = orders_of()
    rounds = []
    for masks in masks_of():
        for turn, mask in masks:
            if mask:
                bit = next(b for b in orders[turn] if (mask >> b) & 1)
                known[turn, mask] = swap(known[turn, mask ^ (1 << bit)], "dp", 1 << bit)
        rounds.append({key: known[key] for key in masks})
    return rounds


def local(momentum, gradient, factor):
    replicas = lax.axis_size("dp")
    moment = momentum[0]
    change = gradient[0]
    all_rows = moment.shape[0] * lax.axis_size("fsdp")
    all_cols = moment.shape[1] * lax.axis_size("tensor")
    left_low = sum_left(left_product(moment, change, factor))
    left_turned = left_low.T
    sides = sides_of()
    mixed = quarters_product(mixed_kernel, 1 - sides, left_turned, moment, change)
    gram, mixed = sum_gram(
        jnp.dot(left_turned, left_low, preferred_element_type=F32), mixed
    )
    inverse, *sent = inverse_and_sent(gram, mixed)
    right = scatter_right(
        sent,
        lambda: quarters_product(kept_kernel, sides, left_turned, moment, change, inverse),
    )
    ortho_low = jnp.dot(
        left_low.astype(F32), inverse.T, precision=lax.Precision.HIGH
    ).astype(LOW)
    places = [places_of(masks) for masks in masks_of()]
    width = right.shape[1] // 2 * lax.axis_size("fsdp")
    moment, change, _ = lax.optimization_barrier((moment, change, inverse))
    moment, change = (
        pltpu.with_memory_space_constraint(x, pltpu.HBM) for x in (moment, change)
    )
    totals = totals_of(places[1:], width, moment, change)
    rounds = gather_rounds(gather_fsdp((right / replicas).astype(LOW)))
    new_momentum = None
    all_pieces = []
    sums = {}
    for r, new in enumerate(rounds):
        for key, piece in new.items():
            wide = piece.astype(F32)
            sums[key] = jnp.sum(wide * wide, axis=1, keepdims=True)
        pieces = jnp.stack(list(new.values()))
        new_momentum = feedback_columns(
            places[r],
            ortho_low,
            pieces,
            moment,
            change,
            totals[r - 1] if r else None,
            new_momentum,
        )
        all_pieces.append(pieces)
    square_sums = tree_sum([sums[key] for key in sorted(sums)])
    for bit in bits_of("tensor"):
        square_sums = square_sums + swap(square_sums, "tensor", 1 << bit)
    norms = jnp.sqrt(square_sums / all_cols + 1e-06)
    scale = (all_rows / factor.shape[1]) ** 0.5
    step_direction, new_factor = step_outputs(
        jnp.concatenate(places), ortho_low, all_pieces, norms, scale
    )
    return (new_momentum, step_direction, new_factor)


def solution(mesh):
    in_specs = (P("dp", "fsdp", "tensor"), P("dp", "fsdp", "tensor"), P("tensor", None))
    out_specs = (P("dp", "fsdp", "tensor"), P("fsdp", "tensor"), P("tensor", None))
    return jax.shard_map(local, mesh=mesh, in_specs=in_specs, out_specs=out_specs, check_vma=False)
```

```python
import functools

import jax
import jax.numpy as jnp
from jax import lax
from jax.experimental import pallas as pl
from jax.experimental.pallas import tpu as pltpu
from jax.sharding import PartitionSpec as P

F32 = jnp.float32
LOW = jnp.bfloat16
LANES = 128
ROOM = 50 << 20
COLS_OVER = (((0,), (0,)), ((), ()))


def inverse_factor_kernel(panel, group, gram_ref, out_ref, work_ref):
    n = gram_ref.shape[0]
    work_ref[...] = jnp.zeros_like(work_ref)
    out_ref[...] = jnp.zeros_like(out_ref)
    rows = lax.broadcasted_iota(jnp.int32, (panel, LANES), 0)
    lanes = lax.broadcasted_iota(jnp.int32, (panel, LANES), 1)
    product = functools.partial(
        lax.dot_general,
        dimension_numbers=COLS_OVER,
        precision=lax.Precision.HIGHEST,
        preferred_element_type=F32,
    )
    for start in range(0, n, panel):
        base = start // LANES * LANES
        wide = base + LANES
        upper = gram_ref[start : start + panel, base:n]
        if start:
            before = work_ref[0:start, start : start + panel]
            upper = upper - product(before, work_ref[0:start, base:n])
            inverse = -product(before, work_ref[0:start, n : n + wide])
            inverse = [inverse[:, c : c + LANES] for c in range(0, wide, LANES)]
        else:
            inverse = [jnp.zeros((panel, LANES), F32)]
        inverse[-1] = inverse[-1] + (lanes == rows + (start - base)).astype(F32)
        upper = [upper[:, c : c + LANES] for c in range(0, n - base, LANES)]
        pivots = jnp.ones((panel, LANES), F32)
        for first in range(0, panel, group):
            lane = start - base + first
            columns = [
                jnp.broadcast_to(upper[0][:, lane + q : lane + q + 1], (panel, LANES))
                for q in range(group)
            ]
            factors = []
            for j in range(group):
                r = first + j
                pivot = columns[j][r : r + 1, :]
                pivots = jnp.where(rows == r, jnp.broadcast_to(pivot, rows.shape), pivots)
                factors.append(jnp.where(rows > r, columns[j] * (1.0 / pivot), 0.0))
                for q in range(j + 1, group):
                    columns[q] = columns[q] - factors[j] * columns[q][r : r + 1, :]
            for j in range(group):
                r = first + j
                upper = [x - factors[j] * x[r : r + 1, :] for x in upper]
                inverse = [x - factors[j] * x[r : r + 1, :] for x in inverse]
        scale = lax.rsqrt(pivots)
        for t, x in enumerate(upper):
            at = base + t * LANES
            work_ref[start : start + panel, at : at + LANES] = x * scale
        for t, x in enumerate(inverse):
            at = t * LANES
            work_ref[start : start + panel, n + at : n + at + LANES] = x * scale
            out_ref[start : start + panel, at : at + LANES] = x * scale


def split_low(x):
    high = x.astype(LOW)
    return high, (x - high.astype(F32)).astype(LOW)


def apply_inverse(inverse, mixed):
    inverse_high, inverse_low = split_low(inverse)
    high, low = split_low(mixed)
    return (
        jnp.dot(inverse_high, low, preferred_element_type=F32)
        + jnp.dot(inverse_low, high, preferred_element_type=F32)
    ) + jnp.dot(inverse_high, high, preferred_element_type=F32)


def sent_kernel(gram_ref, mixed_ref, inverse_ref, first_ref, second_ref, work_ref):
    inverse_factor_kernel(32, 16, gram_ref, inverse_ref, work_ref)
    inverse = inverse_ref[...]
    size = first_ref.shape[1]
    width = tile_of(size)
    for turn, out_ref in enumerate((first_ref, second_ref)):
        for at in range(0, size, width):
            mixed = mixed_ref[:, turn * size + at : turn * size + at + width]
            out_ref[:, at : at + width] = apply_inverse(inverse, mixed).astype(LOW)


def mixed_of(left_ref, moment_ref, change_ref):
    left = left_ref[...]
    return jnp.dot(left, moment_ref[...], preferred_element_type=F32) + jnp.dot(
        left, change_ref[...], preferred_element_type=F32
    )


def mixed_kernel(side_ref, left_ref, moment_ref, change_ref, out_ref):
    out_ref[...] = mixed_of(left_ref, moment_ref, change_ref)


def kept_kernel(side_ref, left_ref, moment_ref, change_ref, inverse_ref, out_ref):
    mixed = mixed_of(left_ref, moment_ref, change_ref)
    out_ref[...] = apply_inverse(inverse_ref[...], mixed)


WHOLE = pl.BlockSpec(memory_space=pltpu.VMEM)


def quarters_product(body, side, left_turned, moment, change, *operands):
    rank, rows = left_turned.shape
    columns = moment.shape[1]
    tile = min(columns // 4, 512)
    steps = columns // 4 // tile

    def place(j, side):
        return (0, (2 * (j // steps) + side[j // steps]) * steps + j % steps)

    block = pl.BlockSpec((rows, tile), place)
    return pl.pallas_call(
        body,
        grid_spec=pltpu.PrefetchScalarGridSpec(
            num_scalar_prefetch=1,
            grid=(2 * steps,),
            in_specs=[pl.BlockSpec((rank, rows), lambda j, side: (0, 0)), block, block]
            + [WHOLE] * len(operands),
            out_specs=pl.BlockSpec((rank, tile), lambda j, side: (0, j)),
        ),
        out_shape=jax.ShapeDtypeStruct((rank, columns // 2), F32),
        compiler_params=pltpu.CompilerParams(vmem_limit_bytes=ROOM),
    )(side, left_turned, moment, change, *operands)


def inverse_and_sent(gram, mixed):
    n, columns = mixed.shape
    quarter = jax.ShapeDtypeStruct((n, columns // 2), LOW)
    return pl.pallas_call(
        sent_kernel,
        out_shape=(jax.ShapeDtypeStruct((n, n), F32), quarter, quarter),
        scratch_shapes=[pltpu.VMEM((n, 2 * n), F32)],
        compiler_params=pltpu.CompilerParams(vmem_limit_bytes=16 << 20),
    )(gram, mixed)


def tile_of(size):
    return 256 if size % 256 == 0 else LANES


def left_kernel(moment_ref, change_ref, factor_ref, out_ref, low_ref):
    @pl.when(pl.program_id(0) == 0)
    def _():
        low_ref[...] = factor_ref[...].astype(LOW)

    factor = low_ref[...]
    out_ref[...] = jnp.dot(moment_ref[...], factor, preferred_element_type=F32) + jnp.dot(
        change_ref[...], factor, preferred_element_type=F32
    )


def left_product(moment, change, factor):
    rows, columns = moment.shape
    rank = factor.shape[1]
    tile = min(rows, 512)
    return pl.pallas_call(
        left_kernel,
        grid=(rows // tile,),
        in_specs=[
            pl.BlockSpec((tile, columns), lambda i: (i, 0)),
            pl.BlockSpec((tile, columns), lambda i: (i, 0)),
            pl.BlockSpec((columns, rank), lambda i: (0, 0), pipeline_mode=pl.Buffered(1)),
        ],
        out_specs=pl.BlockSpec((tile, rank), lambda i: (i, 0)),
        out_shape=jax.ShapeDtypeStruct((rows, rank), F32),
        scratch_shapes=[pltpu.VMEM((columns, rank), LOW)],
        compiler_params=pltpu.CompilerParams(vmem_limit_bytes=ROOM),
        cost_estimate=pl.CostEstimate(
            flops=4 * rows * columns * rank,
            bytes_accessed=4 * rows * columns,
            transcendentals=0,
        ),
    )(moment, change, factor)


def total_kernel(counts, place_ref, moment_ref, change_ref, *out_refs):
    j = pl.program_id(0)
    width = moment_ref.shape[1]
    first = 0
    for count, out_ref in zip(counts, out_refs):

        @pl.when((j >= first) & (j < first + count))
        def _():
            at = jnp.clip(j - first, 0, count - 1) * width
            out_ref[:, pl.ds(pl.multiple_of(at, width), width)] = moment_ref[...].astype(
                F32
            ) + change_ref[...].astype(F32)

        first += count


def totals_of(places, width, moment, change):
    rows = moment.shape[0]
    counts = [place.shape[0] for place in places]
    block = pl.BlockSpec((rows, width), lambda j, place: (0, place[j]))
    return pl.pallas_call(
        functools.partial(total_kernel, counts),
        grid_spec=pltpu.PrefetchScalarGridSpec(
            num_scalar_prefetch=1,
            grid=(sum(counts),),
            in_specs=[block, block],
            out_specs=[WHOLE] * len(counts),
        ),
        out_shape=[pltpu.VMEM((rows, count * width), F32) for count in counts],
        compiler_params=pltpu.CompilerParams(vmem_limit_bytes=14 << 20),
    )(jnp.concatenate(places), moment, change)


def first_kernel(place_ref, ortho_ref, right_ref, moment_ref, change_ref, out_ref):
    feedback = jnp.dot(ortho_ref[...], right_ref[0], preferred_element_type=F32)
    out_ref[0] = moment_ref[...].astype(F32) + change_ref[...].astype(F32) - 0.05 * feedback


def later_kernel(place_ref, ortho_ref, right_ref, total_ref, written_ref, out_ref):
    width = out_ref.shape[2]
    at = pl.multiple_of(pl.program_id(0) * width, width)
    feedback = jnp.dot(ortho_ref[...], right_ref[0], preferred_element_type=F32)
    out_ref[0] = total_ref[:, pl.ds(at, width)] - 0.05 * feedback


def feedback_columns(places, ortho_low, pieces, moment, change, total, written):
    count, rank, width = pieces.shape
    rows, columns = moment.shape
    specs = [WHOLE, pl.BlockSpec((1, rank, width), lambda j, place: (j, 0, 0))]
    if written is None:
        tile = tile_of(width)
        steps = width // tile
        specs[1] = pl.BlockSpec((1, rank, tile), lambda j, place: (j // steps, 0, j % steps))
        block = pl.BlockSpec(
            (rows, tile), lambda j, place: (0, place[j // steps] * steps + j % steps)
        )
        specs += [block, block]
        operands = [moment, change]
        aliases = {}
    else:
        tile, steps = width, 1
        specs += [WHOLE, pl.BlockSpec(memory_space=pl.ANY)]
        operands = [total, written]
        aliases = {4: 0}
    return pl.pallas_call(
        first_kernel if written is None else later_kernel,
        grid_spec=pltpu.PrefetchScalarGridSpec(
            num_scalar_prefetch=1,
            grid=(count * steps,),
            in_specs=specs,
            out_specs=pl.BlockSpec(
                (1, rows, tile), lambda j, place: (0, 0, place[j // steps] * steps + j % steps)
            ),
        ),
        out_shape=jax.ShapeDtypeStruct((1, rows, columns), F32),
        input_output_aliases=aliases,
        compiler_params=pltpu.CompilerParams(vmem_limit_bytes=12 << 20),
    )(places, ortho_low, pieces, *operands)


def step_kernel(scale, counts, place_ref, ortho_ref, *refs):
    norm_ref, step_ref, factor_ref, work_ref = refs[len(counts) :]
    j = pl.program_id(0)
    start = 0
    for count, right_ref in zip(counts, refs):

        @pl.when((j >= start) & (j < start + count))
        def _():
            work_ref[...] = right_ref[0].astype(F32) / norm_ref[...]

        start += count
    factor = work_ref[...]
    product = jnp.dot(ortho_ref[...], factor.astype(LOW), preferred_element_type=F32)
    step_ref[...] = (scale * product).astype(LOW)
    factor_ref[...] = factor.T


def step_outputs(places, ortho_low, rounds, norms, scale):
    counts = [pieces.shape[0] for pieces in rounds]
    starts = [sum(counts[:r]) for r in range(len(counts))]
    _, rank, width = rounds[0].shape
    rows = ortho_low.shape[0]
    columns = sum(counts) * width

    def piece_block(start, count):
        return pl.BlockSpec(
            (1, rank, width), lambda j, place: (jnp.clip(j - start, 0, count - 1), 0, 0)
        )

    return pl.pallas_call(
        functools.partial(step_kernel, scale, counts),
        grid_spec=pltpu.PrefetchScalarGridSpec(
            num_scalar_prefetch=1,
            grid=(sum(counts),),
            in_specs=[WHOLE]
            + [piece_block(start, count) for start, count in zip(starts, counts)]
            + [pl.BlockSpec((rank, 1), lambda j, place: (0, 0))],
            out_specs=[
                pl.BlockSpec((rows, width), lambda j, place: (0, place[j])),
                pl.BlockSpec((width, rank), lambda j, place: (place[j], 0)),
            ],
            scratch_shapes=[pltpu.VMEM((rank, width), F32)],
        ),
        out_shape=[
            jax.ShapeDtypeStruct((rows, columns), LOW),
            jax.ShapeDtypeStruct((columns, rank), F32),
        ],
        compiler_params=pltpu.CompilerParams(vmem_limit_bytes=16 << 20),
    )(
        places,
        ortho_low,
        *(pltpu.with_memory_space_constraint(pieces, pltpu.HBM) for pieces in rounds),
        norms,
    )


def bits_of(axis):
    return range(lax.axis_size(axis).bit_length() - 1)


def swap(x, axis, mask):
    size = lax.axis_size(axis)
    return lax.ppermute(x, axis, [(i, i ^ mask) for i in range(size)])


def halve(x, axis, bit, dtype, dim):
    mine = (lax.axis_index(axis) >> bit) & 1
    size = x.shape[dim] // 2
    kept = lax.dynamic_slice_in_dim(x, mine * size, size, dim)
    sent = lax.dynamic_slice_in_dim(x, (1 - mine) * size, size, dim)
    return kept + swap(sent.astype(dtype), axis, 1 << bit).astype(F32)


def unhalve(x, axis, bit):
    mine = (lax.axis_index(axis) >> bit) & 1
    other = swap(x, axis, 1 << bit)
    return jnp.where(mine == 0, jnp.concatenate([x, other]), jnp.concatenate([other, x]))


def add_both(x, axis, bit):
    low = x.astype(LOW)
    return low.astype(F32) + swap(low, axis, 1 << bit).astype(F32)


def tree_sum(terms):
    while len(terms) > 1:
        terms = [terms[i] + terms[i + 1] for i in range(0, len(terms), 2)]
    return terms[0]


def sum_left(partial):
    for bit in bits_of("tensor"):
        partial = halve(partial, "tensor", bit, F32, 0)
    half = partial.shape[0] // 2
    parts = [partial[:half], partial[half:]]
    bits = list(bits_of("dp"))
    for k in range(len(bits)):
        parts = [
            add_both(part, "dp", bits[(k + turn) % len(bits)]) for turn, part in enumerate(parts)
        ]
    low = (jnp.concatenate(parts) / lax.axis_size("dp")).astype(LOW)
    for bit in reversed(bits_of("tensor")):
        low = unhalve(low, "tensor", bit)
    return low


def sum_gram(gram, mixed):
    shards = lax.axis_size("tensor")
    count = gram.shape[0] // shards
    part = lax.dynamic_slice_in_dim(gram, lax.axis_index("tensor") * count, count, 0)
    part = tree_sum([part] + [swap(part, "fsdp", k) for k in range(1, lax.axis_size("fsdp"))])
    part, mixed = lax.optimization_barrier((part, mixed))
    for bit in bits_of("tensor"):
        part = unhalve(part, "tensor", bit)
    return part, mixed


def orders_of():
    bits = list(bits_of("dp"))
    return [bits[turn % len(bits) :] + bits[: turn % len(bits)] for turn in range(2)]


def sides_of():
    index = lax.axis_index("dp")
    return jnp.stack([(index >> order[0]) & 1 for order in orders_of()])


def scatter_right(sent, keep):
    orders = orders_of()
    come = [swap(x, "dp", 1 << order[0]) for x, order in zip(sent, orders)]
    kept = keep()
    size = kept.shape[1] // 2
    parts = [a + b.astype(F32) for a, b in zip((kept[:, :size], kept[:, size:]), come)]
    for k in range(1, len(orders[0])):
        parts = [
            halve(part, "dp", order[k], LOW, 1) for part, order in zip(parts, orders)
        ]
    size = lax.axis_size("fsdp")
    index = lax.axis_index("fsdp")
    width = parts[0].shape[1] // size

    def share(at):
        return jnp.concatenate(
            [lax.dynamic_slice_in_dim(part, at * width, width, 1) for part in parts], axis=1
        )

    terms = [share(index)]
    for k in range(1, size):
        terms.append(swap(share(index ^ k).astype(LOW), "fsdp", k).astype(F32))
    return tree_sum(terms)


def gather_fsdp(low):
    size = lax.axis_size("fsdp")
    index = lax.axis_index("fsdp")
    width = low.shape[1] // 2
    blocks = [low] + [swap(low, "fsdp", k) for k in range(1, size)]
    for bit in bits_of("fsdp"):
        high = ((index >> bit) & 1) == 1
        blocks = [jnp.where(high, blocks[i ^ (1 << bit)], blocks[i]) for i in range(size)]
    return [
        jnp.concatenate([b[:, :width] for b in blocks], axis=1),
        jnp.concatenate([b[:, width:] for b in blocks], axis=1),
    ]


def masks_of():
    depth = len(orders_of()[0])
    return [
        [(turn, mask) for turn in range(2) for mask in range(1 << depth) if mask.bit_count() == r]
        for r in range(depth + 1)
    ]


def places_of(masks):
    index = lax.axis_index("dp")
    orders = orders_of()
    depth = len(orders[0])
    places = []
    for turn, mask in masks:
        place = jnp.int32(turn << depth)
        for k, b in enumerate(orders[turn]):
            place = place + ((((index ^ mask) >> b) & 1) << (depth - 1 - k))
        places.append(place)
    return jnp.stack(places)


def gather_rounds(pieces):
    known = {(turn, 0): piece for turn, piece in enumerate(pieces)}
    orders = orders_of()
    rounds = []
    for masks in masks_of():
        for turn, mask in masks:
            if mask:
                bit = next(b for b in orders[turn] if (mask >> b) & 1)
                known[turn, mask] = swap(known[turn, mask ^ (1 << bit)], "dp", 1 << bit)
        rounds.append({key: known[key] for key in masks})
    return rounds


def local(momentum, gradient, factor):
    replicas = lax.axis_size("dp")
    moment = momentum[0]
    change = gradient[0]
    all_rows = moment.shape[0] * lax.axis_size("fsdp")
    all_cols = moment.shape[1] * lax.axis_size("tensor")
    left_low = sum_left(left_product(moment, change, factor))
    left_turned = left_low.T
    sides = sides_of()
    mixed = quarters_product(mixed_kernel, 1 - sides, left_turned, moment, change)
    gram, mixed = sum_gram(
        jnp.dot(left_turned, left_low, preferred_element_type=F32), mixed
    )
    inverse, *sent = inverse_and_sent(gram, mixed)
    right = scatter_right(
        sent,
        lambda: quarters_product(kept_kernel, sides, left_turned, moment, change, inverse),
    )
    ortho_low = jnp.dot(
        left_low.astype(F32), inverse.T, precision=lax.Precision.HIGH
    ).astype(LOW)
    places = [places_of(masks) for masks in masks_of()]
    width = right.shape[1] // 2 * lax.axis_size("fsdp")
    moment, change, _ = lax.optimization_barrier((moment, change, inverse))
    moment, change = (
        pltpu.with_memory_space_constraint(x, pltpu.HBM) for x in (moment, change)
    )
    totals = totals_of(places[1:], width, moment, change)
    rounds = gather_rounds(gather_fsdp((right / replicas).astype(LOW)))
    new_momentum = None
    all_pieces = []
    sums = {}
    for r, new in enumerate(rounds):
        for key, piece in new.items():
            wide = piece.astype(F32)
            sums[key] = jnp.sum(wide * wide, axis=1, keepdims=True)
        pieces = jnp.stack(list(new.values()))
        new_momentum = feedback_columns(
            places[r],
            ortho_low,
            pieces,
            moment,
            change,
            totals[r - 1] if r else None,
            new_momentum,
        )
        all_pieces.append(pieces)
    square_sums = tree_sum([sums[key] for key in sorted(sums)])
    for bit in bits_of("tensor"):
        square_sums = square_sums + swap(square_sums, "tensor", 1 << bit)
    norms = jnp.sqrt(square_sums / all_cols + 1e-06)
    scale = (all_rows / factor.shape[1]) ** 0.5
    step_direction, new_factor = step_outputs(
        jnp.concatenate(places), ortho_low, all_pieces, norms, scale
    )
    return (new_momentum, step_direction, new_factor)


def solution(mesh):
    in_specs = (P("dp", "fsdp", "tensor"), P("dp", "fsdp", "tensor"), P("tensor", None))
    out_specs = (P("dp", "fsdp", "tensor"), P("fsdp", "tensor"), P("tensor", None))
    return jax.shard_map(local, mesh=mesh, in_specs=in_specs, out_specs=out_specs, check_vma=False)
```

```python
import functools

import jax
import jax.numpy as jnp
from jax import lax
from jax.experimental import pallas as pl
from jax.experimental.pallas import tpu as pltpu
from jax.sharding import PartitionSpec as P

F32 = jnp.float32
LOW = jnp.bfloat16
LANES = 128
ROOM = 50 << 20
COLS_OVER = (((0,), (0,)), ((), ()))


def inverse_factor_kernel(panel, group, gram_ref, out_ref, work_ref):
    n = gram_ref.shape[0]
    work_ref[...] = jnp.zeros_like(work_ref)
    out_ref[...] = jnp.zeros_like(out_ref)
    rows = lax.broadcasted_iota(jnp.int32, (panel, LANES), 0)
    lanes = lax.broadcasted_iota(jnp.int32, (panel, LANES), 1)
    dot = functools.partial(
        lax.dot_general, dimension_numbers=COLS_OVER, preferred_element_type=F32
    )

    def product(x, y):
        x_high, x_low = split_low(x)
        y_high, y_low = split_low(y)
        return (dot(x_high, y_low) + dot(x_low, y_high)) + dot(x_high, y_high)

    for start in range(0, n, panel):
        base = start // LANES * LANES
        wide = base + LANES
        upper = gram_ref[start : start + panel, base:n]
        if start:
            before = work_ref[0:start, start : start + panel]
            upper = upper - product(before, work_ref[0:start, base:n])
            inverse = -product(before, work_ref[0:start, n : n + wide])
            inverse = [inverse[:, c : c + LANES] for c in range(0, wide, LANES)]
        else:
            inverse = [jnp.zeros((panel, LANES), F32)]
        inverse[-1] = inverse[-1] + (lanes == rows + (start - base)).astype(F32)
        upper = [upper[:, c : c + LANES] for c in range(0, n - base, LANES)]
        pivots = jnp.ones((panel, LANES), F32)
        for first in range(0, panel, group):
            lane = start - base + first
            columns = [
                jnp.broadcast_to(upper[0][:, lane + q : lane + q + 1], (panel, LANES))
                for q in range(group)
            ]
            factors = []
            for j in range(group):
                r = first + j
                pivot = columns[j][r : r + 1, :]
                pivots = jnp.where(rows == r, jnp.broadcast_to(pivot, rows.shape), pivots)
                factors.append(jnp.where(rows > r, columns[j] * (1.0 / pivot), 0.0))
                for q in range(j + 1, group):
                    columns[q] = columns[q] - factors[j] * columns[q][r : r + 1, :]
            for j in range(group):
                r = first + j
                upper = [x - factors[j] * x[r : r + 1, :] for x in upper]
                inverse = [x - factors[j] * x[r : r + 1, :] for x in inverse]
        scale = lax.rsqrt(pivots)
        for t, x in enumerate(upper):
            at = base + t * LANES
            work_ref[start : start + panel, at : at + LANES] = x * scale
        for t, x in enumerate(inverse):
            at = t * LANES
            work_ref[start : start + panel, n + at : n + at + LANES] = x * scale
            out_ref[start : start + panel, at : at + LANES] = x * scale


def split_low(x):
    high = x.astype(LOW)
    return high, (x - high.astype(F32)).astype(LOW)


def apply_inverse(inverse, mixed):
    inverse_high, inverse_low = split_low(inverse)
    high, low = split_low(mixed)
    return (
        jnp.dot(inverse_high, low, preferred_element_type=F32)
        + jnp.dot(inverse_low, high, preferred_element_type=F32)
    ) + jnp.dot(inverse_high, high, preferred_element_type=F32)


def sent_kernel(gram_ref, mixed_ref, inverse_ref, first_ref, second_ref, work_ref):
    inverse_factor_kernel(32, 16, gram_ref, inverse_ref, work_ref)
    inverse = inverse_ref[...]
    size = first_ref.shape[1]
    width = tile_of(size)
    for turn, out_ref in enumerate((first_ref, second_ref)):
        for at in range(0, size, width):
            mixed = mixed_ref[:, turn * size + at : turn * size + at + width]
            out_ref[:, at : at + width] = apply_inverse(inverse, mixed).astype(LOW)


def mixed_of(left_ref, moment_ref, change_ref):
    left = left_ref[...]
    return jnp.dot(left, moment_ref[...], preferred_element_type=F32) + jnp.dot(
        left, change_ref[...], preferred_element_type=F32
    )


def mixed_kernel(side_ref, left_ref, moment_ref, change_ref, out_ref):
    out_ref[...] = mixed_of(left_ref, moment_ref, change_ref)


def kept_kernel(side_ref, left_ref, moment_ref, change_ref, inverse_ref, out_ref):
    mixed = mixed_of(left_ref, moment_ref, change_ref)
    out_ref[...] = apply_inverse(inverse_ref[...], mixed)


WHOLE = pl.BlockSpec(memory_space=pltpu.VMEM)


def quarters_product(body, side, left_turned, moment, change, *operands):
    rank, rows = left_turned.shape
    columns = moment.shape[1]
    tile = min(columns // 4, 512)
    steps = columns // 4 // tile

    def place(j, side):
        return (0, (2 * (j // steps) + side[j // steps]) * steps + j % steps)

    block = pl.BlockSpec((rows, tile), place)
    return pl.pallas_call(
        body,
        grid_spec=pltpu.PrefetchScalarGridSpec(
            num_scalar_prefetch=1,
            grid=(2 * steps,),
            in_specs=[pl.BlockSpec((rank, rows), lambda j, side: (0, 0)), block, block]
            + [WHOLE] * len(operands),
            out_specs=pl.BlockSpec((rank, tile), lambda j, side: (0, j)),
        ),
        out_shape=jax.ShapeDtypeStruct((rank, columns // 2), F32),
        compiler_params=pltpu.CompilerParams(vmem_limit_bytes=ROOM),
    )(side, left_turned, moment, change, *operands)


def inverse_and_sent(gram, mixed):
    n, columns = mixed.shape
    quarter = jax.ShapeDtypeStruct((n, columns // 2), LOW)
    return pl.pallas_call(
        sent_kernel,
        out_shape=(jax.ShapeDtypeStruct((n, n), F32), quarter, quarter),
        scratch_shapes=[pltpu.VMEM((n, 2 * n), F32)],
        compiler_params=pltpu.CompilerParams(vmem_limit_bytes=16 << 20),
    )(gram, mixed)


def tile_of(size):
    return 256 if size % 256 == 0 else LANES


def left_kernel(moment_ref, change_ref, factor_ref, out_ref, low_ref):
    @pl.when(pl.program_id(0) == 0)
    def _():
        low_ref[...] = factor_ref[...].astype(LOW)

    factor = low_ref[...]
    out_ref[...] = jnp.dot(moment_ref[...], factor, preferred_element_type=F32) + jnp.dot(
        change_ref[...], factor, preferred_element_type=F32
    )


def left_product(moment, change, factor):
    rows, columns = moment.shape
    rank = factor.shape[1]
    tile = min(rows, 512)
    return pl.pallas_call(
        left_kernel,
        grid=(rows // tile,),
        in_specs=[
            pl.BlockSpec((tile, columns), lambda i: (i, 0)),
            pl.BlockSpec((tile, columns), lambda i: (i, 0)),
            pl.BlockSpec((columns, rank), lambda i: (0, 0), pipeline_mode=pl.Buffered(1)),
        ],
        out_specs=pl.BlockSpec((tile, rank), lambda i: (i, 0)),
        out_shape=jax.ShapeDtypeStruct((rows, rank), F32),
        scratch_shapes=[pltpu.VMEM((columns, rank), LOW)],
        compiler_params=pltpu.CompilerParams(vmem_limit_bytes=ROOM),
        cost_estimate=pl.CostEstimate(
            flops=4 * rows * columns * rank,
            bytes_accessed=4 * rows * columns,
            transcendentals=0,
        ),
    )(moment, change, factor)


def total_kernel(counts, place_ref, moment_ref, change_ref, *out_refs):
    j = pl.program_id(0)
    width = moment_ref.shape[1]
    first = 0
    for count, out_ref in zip(counts, out_refs):

        @pl.when((j >= first) & (j < first + count))
        def _():
            at = jnp.clip(j - first, 0, count - 1) * width
            out_ref[:, pl.ds(pl.multiple_of(at, width), width)] = moment_ref[...].astype(
                F32
            ) + change_ref[...].astype(F32)

        first += count


def totals_of(places, width, moment, change):
    rows = moment.shape[0]
    counts = [place.shape[0] for place in places]
    block = pl.BlockSpec((rows, width), lambda j, place: (0, place[j]))
    return pl.pallas_call(
        functools.partial(total_kernel, counts),
        grid_spec=pltpu.PrefetchScalarGridSpec(
            num_scalar_prefetch=1,
            grid=(sum(counts),),
            in_specs=[block, block],
            out_specs=[WHOLE] * len(counts),
        ),
        out_shape=[pltpu.VMEM((rows, count * width), F32) for count in counts],
        compiler_params=pltpu.CompilerParams(vmem_limit_bytes=14 << 20),
    )(jnp.concatenate(places), moment, change)


def first_kernel(place_ref, ortho_ref, right_ref, moment_ref, change_ref, out_ref):
    feedback = jnp.dot(ortho_ref[...], right_ref[0], preferred_element_type=F32)
    out_ref[0] = moment_ref[...].astype(F32) + change_ref[...].astype(F32) - 0.05 * feedback


def later_kernel(place_ref, ortho_ref, right_ref, total_ref, written_ref, out_ref):
    width = out_ref.shape[2]
    at = pl.multiple_of(pl.program_id(0) * width, width)
    feedback = jnp.dot(ortho_ref[...], right_ref[0], preferred_element_type=F32)
    out_ref[0] = total_ref[:, pl.ds(at, width)] - 0.05 * feedback


def feedback_columns(places, ortho_low, pieces, moment, change, total, written):
    count, rank, width = pieces.shape
    rows, columns = moment.shape
    specs = [WHOLE, pl.BlockSpec((1, rank, width), lambda j, place: (j, 0, 0))]
    if written is None:
        tile = tile_of(width)
        steps = width // tile
        specs[1] = pl.BlockSpec((1, rank, tile), lambda j, place: (j // steps, 0, j % steps))
        block = pl.BlockSpec(
            (rows, tile), lambda j, place: (0, place[j // steps] * steps + j % steps)
        )
        specs += [block, block]
        operands = [moment, change]
        aliases = {}
    else:
        tile, steps = width, 1
        specs += [WHOLE, pl.BlockSpec(memory_space=pl.ANY)]
        operands = [total, written]
        aliases = {4: 0}
    return pl.pallas_call(
        first_kernel if written is None else later_kernel,
        grid_spec=pltpu.PrefetchScalarGridSpec(
            num_scalar_prefetch=1,
            grid=(count * steps,),
            in_specs=specs,
            out_specs=pl.BlockSpec(
                (1, rows, tile), lambda j, place: (0, 0, place[j // steps] * steps + j % steps)
            ),
        ),
        out_shape=jax.ShapeDtypeStruct((1, rows, columns), F32),
        input_output_aliases=aliases,
        compiler_params=pltpu.CompilerParams(vmem_limit_bytes=12 << 20),
    )(places, ortho_low, pieces, *operands)


def step_kernel(scale, counts, place_ref, ortho_ref, *refs):
    norm_ref, step_ref, factor_ref, work_ref = refs[len(counts) :]
    j = pl.program_id(0)
    start = 0
    for count, right_ref in zip(counts, refs):

        @pl.when((j >= start) & (j < start + count))
        def _():
            work_ref[...] = right_ref[0].astype(F32) / norm_ref[...]

        start += count
    factor = work_ref[...]
    product = jnp.dot(ortho_ref[...], factor.astype(LOW), preferred_element_type=F32)
    step_ref[...] = (scale * product).astype(LOW)
    factor_ref[...] = factor.T


def step_outputs(places, ortho_low, rounds, norms, scale):
    counts = [pieces.shape[0] for pieces in rounds]
    starts = [sum(counts[:r]) for r in range(len(counts))]
    _, rank, width = rounds[0].shape
    rows = ortho_low.shape[0]
    columns = sum(counts) * width

    def piece_block(start, count):
        return pl.BlockSpec(
            (1, rank, width), lambda j, place: (jnp.clip(j - start, 0, count - 1), 0, 0)
        )

    return pl.pallas_call(
        functools.partial(step_kernel, scale, counts),
        grid_spec=pltpu.PrefetchScalarGridSpec(
            num_scalar_prefetch=1,
            grid=(sum(counts),),
            in_specs=[WHOLE]
            + [piece_block(start, count) for start, count in zip(starts, counts)]
            + [pl.BlockSpec((rank, 1), lambda j, place: (0, 0))],
            out_specs=[
                pl.BlockSpec((rows, width), lambda j, place: (0, place[j])),
                pl.BlockSpec((width, rank), lambda j, place: (place[j], 0)),
            ],
            scratch_shapes=[pltpu.VMEM((rank, width), F32)],
        ),
        out_shape=[
            jax.ShapeDtypeStruct((rows, columns), LOW),
            jax.ShapeDtypeStruct((columns, rank), F32),
        ],
        compiler_params=pltpu.CompilerParams(vmem_limit_bytes=16 << 20),
    )(
        places,
        ortho_low,
        *(pltpu.with_memory_space_constraint(pieces, pltpu.HBM) for pieces in rounds),
        norms,
    )


def bits_of(axis):
    return range(lax.axis_size(axis).bit_length() - 1)


def swap(x, axis, mask):
    size = lax.axis_size(axis)
    return lax.ppermute(x, axis, [(i, i ^ mask) for i in range(size)])


def halve(x, axis, bit, dtype, dim):
    mine = (lax.axis_index(axis) >> bit) & 1
    size = x.shape[dim] // 2
    kept = lax.dynamic_slice_in_dim(x, mine * size, size, dim)
    sent = lax.dynamic_slice_in_dim(x, (1 - mine) * size, size, dim)
    return kept + swap(sent.astype(dtype), axis, 1 << bit).astype(F32)


def unhalve(x, axis, bit):
    mine = (lax.axis_index(axis) >> bit) & 1
    other = swap(x, axis, 1 << bit)
    return jnp.where(mine == 0, jnp.concatenate([x, other]), jnp.concatenate([other, x]))


def add_both(x, axis, bit):
    low = x.astype(LOW)
    return low.astype(F32) + swap(low, axis, 1 << bit).astype(F32)


def tree_sum(terms):
    while len(terms) > 1:
        terms = [terms[i] + terms[i + 1] for i in range(0, len(terms), 2)]
    return terms[0]


def sum_left(partial):
    for bit in bits_of("tensor"):
        partial = halve(partial, "tensor", bit, F32, 0)
    half = partial.shape[0] // 2
    parts = [partial[:half], partial[half:]]
    bits = list(bits_of("dp"))
    for k in range(len(bits)):
        parts = [
            add_both(part, "dp", bits[(k + turn) % len(bits)]) for turn, part in enumerate(parts)
        ]
    low = (jnp.concatenate(parts) / lax.axis_size("dp")).astype(LOW)
    for bit in reversed(bits_of("tensor")):
        low = unhalve(low, "tensor", bit)
    return low


def sum_gram(gram, mixed):
    shards = lax.axis_size("tensor")
    count = gram.shape[0] // shards
    part = lax.dynamic_slice_in_dim(gram, lax.axis_index("tensor") * count, count, 0)
    part = tree_sum([part] + [swap(part, "fsdp", k) for k in range(1, lax.axis_size("fsdp"))])
    part, mixed = lax.optimization_barrier((part, mixed))
    for bit in bits_of("tensor"):
        part = unhalve(part, "tensor", bit)
    return part, mixed


def orders_of():
    bits = list(bits_of("dp"))
    return [bits[turn % len(bits) :] + bits[: turn % len(bits)] for turn in range(2)]


def sides_of():
    index = lax.axis_index("dp")
    return jnp.stack([(index >> order[0]) & 1 for order in orders_of()])


def scatter_right(sent, keep):
    orders = orders_of()
    come = [swap(x, "dp", 1 << order[0]) for x, order in zip(sent, orders)]
    kept = keep()
    size = kept.shape[1] // 2
    parts = [a + b.astype(F32) for a, b in zip((kept[:, :size], kept[:, size:]), come)]
    for k in range(1, len(orders[0])):
        parts = [
            halve(part, "dp", order[k], LOW, 1) for part, order in zip(parts, orders)
        ]
    size = lax.axis_size("fsdp")
    index = lax.axis_index("fsdp")
    width = parts[0].shape[1] // size

    def share(at):
        return jnp.concatenate(
            [lax.dynamic_slice_in_dim(part, at * width, width, 1) for part in parts], axis=1
        )

    terms = [share(index)]
    for k in range(1, size):
        terms.append(swap(share(index ^ k).astype(LOW), "fsdp", k).astype(F32))
    return tree_sum(terms)


def gather_fsdp(low):
    size = lax.axis_size("fsdp")
    index = lax.axis_index("fsdp")
    width = low.shape[1] // 2
    blocks = [low] + [swap(low, "fsdp", k) for k in range(1, size)]
    for bit in bits_of("fsdp"):
        high = ((index >> bit) & 1) == 1
        blocks = [jnp.where(high, blocks[i ^ (1 << bit)], blocks[i]) for i in range(size)]
    return [
        jnp.concatenate([b[:, :width] for b in blocks], axis=1),
        jnp.concatenate([b[:, width:] for b in blocks], axis=1),
    ]


def masks_of():
    depth = len(orders_of()[0])
    return [
        [(turn, mask) for turn in range(2) for mask in range(1 << depth) if mask.bit_count() == r]
        for r in range(depth + 1)
    ]


def places_of(masks):
    index = lax.axis_index("dp")
    orders = orders_of()
    depth = len(orders[0])
    places = []
    for turn, mask in masks:
        place = jnp.int32(turn << depth)
        for k, b in enumerate(orders[turn]):
            place = place + ((((index ^ mask) >> b) & 1) << (depth - 1 - k))
        places.append(place)
    return jnp.stack(places)


def gather_rounds(pieces):
    known = {(turn, 0): piece for turn, piece in enumerate(pieces)}
    orders = orders_of()
    rounds = []
    for masks in masks_of():
        for turn, mask in masks:
            if mask:
                bit = next(b for b in orders[turn] if (mask >> b) & 1)
                known[turn, mask] = swap(known[turn, mask ^ (1 << bit)], "dp", 1 << bit)
        rounds.append({key: known[key] for key in masks})
    return rounds


def local(momentum, gradient, factor):
    replicas = lax.axis_size("dp")
    moment = momentum[0]
    change = gradient[0]
    all_rows = moment.shape[0] * lax.axis_size("fsdp")
    all_cols = moment.shape[1] * lax.axis_size("tensor")
    left_low = sum_left(left_product(moment, change, factor))
    left_turned = left_low.T
    sides = sides_of()
    mixed = quarters_product(mixed_kernel, 1 - sides, left_turned, moment, change)
    gram, mixed = sum_gram(
        jnp.dot(left_turned, left_low, preferred_element_type=F32), mixed
    )
    inverse, *sent = inverse_and_sent(gram, mixed)
    right = scatter_right(
        sent,
        lambda: quarters_product(kept_kernel, sides, left_turned, moment, change, inverse),
    )
    ortho_low = jnp.dot(
        left_low.astype(F32), inverse.T, precision=lax.Precision.HIGH
    ).astype(LOW)
    places = [places_of(masks) for masks in masks_of()]
    width = right.shape[1] // 2 * lax.axis_size("fsdp")
    moment, change, _ = lax.optimization_barrier((moment, change, inverse))
    moment, change = (
        pltpu.with_memory_space_constraint(x, pltpu.HBM) for x in (moment, change)
    )
    totals = totals_of(places[1:], width, moment, change)
    rounds = gather_rounds(gather_fsdp((right / replicas).astype(LOW)))
    new_momentum = None
    all_pieces = []
    sums = {}
    for r, new in enumerate(rounds):
        for key, piece in new.items():
            wide = piece.astype(F32)
            sums[key] = jnp.sum(wide * wide, axis=1, keepdims=True)
        pieces = jnp.stack(list(new.values()))
        new_momentum = feedback_columns(
            places[r],
            ortho_low,
            pieces,
            moment,
            change,
            totals[r - 1] if r else None,
            new_momentum,
        )
        all_pieces.append(pieces)
    square_sums = tree_sum([sums[key] for key in sorted(sums)])
    for bit in bits_of("tensor"):
        square_sums = square_sums + swap(square_sums, "tensor", 1 << bit)
    norms = jnp.sqrt(square_sums / all_cols + 1e-06)
    scale = (all_rows / factor.shape[1]) ** 0.5
    step_direction, new_factor = step_outputs(
        jnp.concatenate(places), ortho_low, all_pieces, norms, scale
    )
    return (new_momentum, step_direction, new_factor)


def solution(mesh):
    in_specs = (P("dp", "fsdp", "tensor"), P("dp", "fsdp", "tensor"), P("tensor", None))
    out_specs = (P("dp", "fsdp", "tensor"), P("fsdp", "tensor"), P("tensor", None))
    return jax.shard_map(local, mesh=mesh, in_specs=in_specs, out_specs=out_specs, check_vma=False)
```
